128 devices in a mesh: gx: 16 (over z, y), gy: 8 (over x, core).
Axes of the slice: x: 4, y: 4, z: 4, core: 2. Of those that a mesh axis runs over, the one named last changes fastest.
Arguments:
- tokens: bfloat16 [512, 8192], P('gy', 'gx'), may hold values from -400 to 400
- w_query: bfloat16 [8192, 8192], P('gx', 'gy'), may hold values from -0.0625 to 0.0625
- w_key_value: bfloat16 [8192, 512], P('gx', 'gy'), may hold values from -0.0625 to 0.0625
- w_gate: bfloat16 [8192, 32768], P('gx', 'gy'), may hold values from -0.0625 to 0.0625
- w_up: bfloat16 [8192, 32768], P('gx', 'gy'), may hold values from -0.0625 to 0.0625
- w_attn_out: bfloat16 [8192, 8192], P('gy', 'gx'), may hold values from -0.75 to 0.75
- w_down: bfloat16 [32768, 8192], P('gy', 'gx'), may hold values from -0.03125 to 0.03125
- key_cache: bfloat16 [512, 2048, 256], P(('gx', 'gy')), may hold values from -1000 to 1000
- value_cache: bfloat16 [512, 2048, 256], P(('gx', 'gy')), may hold values from -6 to 6
Outputs:
- layer_out: bfloat16 [512, 8192], P('gy', 'gx')
- new_kv: bfloat16 [512, 512], P(('gx', 'gy'))
The draws below stay inside these ranges and needn't reach their ends.
All inputs are finite; a program needn't handle non-finite values.
Results may differ from the reference program's by a relative error of at most 0.035.
Values may be sent and summed in bfloat16 or wider, within the bound.
No kernel may reach another device: no remote copies, remote signals or barrier semaphores. Data moves between devices by JAX's collectives and lax.ppermute only.
A program may use at most 128 MiB of HBM per device.

```python
import jax
import jax.numpy as jnp
from jax import lax

D = 8192
HEADS = 32
HD = 256
FF = 32768
CACHE = 2048
ROWS = 512
N_GX = 16


def draw_tokens(key, part):
    key = jax.random.fold_in(key, 5)
    first = jax.random.fold_in(key, 0)
    base = jnp.clip(jax.random.normal(first, (ROWS, D), jnp.float32), -6.0, 6.0)
    column = jnp.arange(D, dtype=jnp.float32) / (D - 1)
    rising = 1.0 + 2.0 * column
    values = base * rising
    return jnp.clip(values, -400.0, 400.0).astype(jnp.bfloat16)


def draw_key_cache(key, part):
    key = jax.random.fold_in(key, 11)
    first = jax.random.fold_in(key, 0)
    base = jnp.clip(jax.random.normal(first, (ROWS, CACHE, HD), jnp.float32), -6.0, 6.0)
    values = base
    return jnp.clip(values, -1000.0, 1000.0).astype(jnp.bfloat16)


def block_levels(own_key, dims, pieces, low, high):
    factor_of = 1.0
    for dim, parts in pieces:
        draws = jax.random.uniform(jax.random.fold_in(jax.random.fold_in(own_key, 6), dim), (parts,), jnp.float32, low / len(pieces), high / len(pieces))
        factor_of = factor_of * jnp.repeat(jnp.exp(draws), dims[dim] // parts).reshape((-1,) + (1,) * (len(dims) - 1 - dim))
    return factor_of


def scatter_about(stream_key, extent, deviation, limit, shards=(), kind=jnp.bfloat16):
    level = block_levels(stream_key, extent, shards, -0.22, 0.18) if shards else 1.0
    result = jax.random.normal(stream_key, extent, jnp.float32) * deviation * level
    return jnp.minimum(jnp.maximum(result, -limit), limit).astype(kind)


def setup_inputs(seed: int = 0) -> dict:
    splits = jax.random.split(jax.random.key(seed), 10)
    tokens = draw_tokens(jax.random.fold_in(splits[9], 71), 0)
    w_query = scatter_about(splits[1], (D, HEADS * HD), D ** -0.5, 0.0625, ((0, 16), (1, 8)))
    w_key_value = scatter_about(splits[2], (D, 2 * HD), D ** -0.5, 0.0625, ((0, 16), (1, 8)))
    w_gate = scatter_about(splits[3], (D, FF), D ** -0.5, 0.0625, ((0, 16), (1, 8)))
    w_up = scatter_about(splits[4], (D, FF), D ** -0.5, 0.0625, ((0, 16), (1, 8)))
    w_attn_out = scatter_about(splits[5], (HEADS * HD, D), (HD // 4) ** -0.5, 0.75, ((0, 8), (1, 16)))
    w_down = scatter_about(splits[6], (FF, D), FF ** -0.5, 0.03125, ((0, 8), (1, 16)))
    key_cache = draw_key_cache(jax.random.fold_in(splits[9], 71), 0)
    value_cache = scatter_about(splits[8], (ROWS, CACHE, HD), 1.0, 6.0, ((0, 128),))
    return {"tokens": tokens, "w_query": w_query, "w_key_value": w_key_value, "w_gate": w_gate, "w_up": w_up, "w_attn_out": w_attn_out, "w_down": w_down, "key_cache": key_cache, "value_cache": value_cache}


def rotate(values, cos_part, sin_part):
    half = values.shape[-1] // 2
    first = values[..., :half]
    second = values[..., half:]
    return jnp.concatenate([first * cos_part - second * sin_part, first * sin_part + second * cos_part], axis=-1)

def block_sum(normed, weight):
    width = D // N_GX

    def add_block(index, total):
        start = (index * width).astype(jnp.int32)
        rows = lax.dynamic_slice_in_dim(normed, start, width, 1)
        cols = lax.dynamic_slice_in_dim(weight, start, width, 0)
        partial_sum = jnp.dot(rows, cols, preferred_element_type=jnp.float32).astype(jnp.bfloat16)
        partial_sum = lax.optimization_barrier(partial_sum)
        return total + partial_sum.astype(jnp.float32)
    empty = jnp.zeros((normed.shape[0], weight.shape[1]), jnp.float32)
    return lax.fori_loop(jnp.int32(0), jnp.int32(N_GX), add_block, empty)

def reference(tokens, w_query, w_key_value, w_gate, w_up, w_attn_out, w_down, key_cache, value_cache):
    values = tokens.astype(jnp.float32)
    mean = lax.optimization_barrier(jnp.sum(values, axis=1, keepdims=True)) / D
    centered = values - mean
    spread = lax.optimization_barrier(jnp.sum(centered * centered, axis=1, keepdims=True)) / D
    normed = (centered * lax.rsqrt(spread + 1e-05)).astype(jnp.bfloat16)
    query = block_sum(normed, w_query).astype(jnp.bfloat16)
    keyval = block_sum(normed, w_key_value).astype(jnp.bfloat16)
    gate = block_sum(normed, w_gate)
    upper = block_sum(normed, w_up)
    hidden = (jax.nn.silu(gate) * upper).astype(jnp.bfloat16)
    half = HD // 2
    freqs = 10000.0 ** (-jnp.arange(half, dtype=jnp.float32) / half)
    angles = jnp.float32(CACHE) * freqs
    cos_part = jnp.cos(angles)
    sin_part = jnp.sin(angles)
    heads_in = query.reshape(ROWS, HEADS, HD).astype(jnp.float32)
    qrot = (rotate(heads_in, cos_part, sin_part) * HD ** (-0.5)).astype(jnp.bfloat16)
    krot = rotate(keyval[:, :HD].astype(jnp.float32), cos_part, sin_part).astype(jnp.bfloat16)
    new_value = keyval[:, HD:]
    new_kv = jnp.concatenate([krot, new_value], axis=1)

    def one_row(items):
        q_row, k_row, v_row, keys, vals = items
        q32 = q_row.astype(jnp.float32)
        scores = jnp.einsum('hd,td->ht', q32, keys.astype(jnp.float32))
        own = jnp.einsum('hd,d->h', q32, k_row.astype(jnp.float32))
        top = jnp.maximum(lax.optimization_barrier(jnp.max(scores, axis=1)), own)
        weights = jnp.exp(scores - top[:, None])
        own_w = jnp.exp(own - top)
        total = lax.optimization_barrier(jnp.sum(weights, axis=1)) + own_w
        probs = (weights / total[:, None]).astype(jnp.bfloat16)
        own_p = (own_w / total).astype(jnp.bfloat16)
        mixed = jnp.einsum('ht,td->hd', probs.astype(jnp.float32), vals.astype(jnp.float32))
        mixed = mixed + own_p.astype(jnp.float32)[:, None] * v_row.astype(jnp.float32)[None, :]
        return mixed.reshape(HEADS * HD).astype(jnp.bfloat16)
    attended = lax.map(one_row, (qrot, krot, new_value, key_cache, value_cache))
    branch = jnp.dot(attended, w_attn_out, preferred_element_type=jnp.float32)
    branch = branch + jnp.dot(hidden, w_down, preferred_element_type=jnp.float32)
    layer_out = (values + branch).astype(jnp.bfloat16)
    return (layer_out, new_kv)
```

```python
import functools

import jax
import jax.numpy as jnp
from jax import lax
from jax.experimental import pallas as pl
from jax.experimental.pallas import tpu as pltpu
from jax.sharding import PartitionSpec as P

D = 8192
HEADS = 32
HD = 256
NZ = 4
NY = 4
NX = 4
CHUNK = 32
QUARTER = 128
BLOCK = 512
HID_Z = 2048
F32 = jnp.float32
BF16 = jnp.bfloat16
VMEM = pl.BlockSpec(memory_space=pltpu.VMEM)


def ring_y(shift):
    return [(z * NY + y, z * NY + (y + shift) % NY) for z in range(NZ) for y in range(NY)]


def ring_z(shift):
    return [(z * NY + y, ((z + shift) % NZ) * NY + y) for z in range(NZ) for y in range(NY)]


def ring_x(shift):
    return [(x * 2 + c, ((x + shift) % NX) * 2 + c) for x in range(NX) for c in range(2)]


CORES = [(x * 2 + c, x * 2 + 1 - c) for x in range(NX) for c in range(2)]


def send(value, pairs, axis="gx"):
    return lax.ppermute(value, axis, pairs)


def send_direct(chunks, ring, axis="gx"):
    return (
        send(chunks[1], ring(1), axis),
        send(chunks[3], ring(-1), axis),
        send(chunks[2], ring(2), axis),
    )


def gather_direct(value, ring, axis="gx"):
    left, right, far = send_direct([value] * 4, ring, axis)
    return [value, right, far, left]


def add(*values):
    total = values[0].astype(F32)
    for value in values[1:]:
        total = total + value.astype(F32)
    return total


def dot(a, b):
    return jnp.dot(a, b, preferred_element_type=F32)


def roll(values, axis, shift):
    size = values.shape[axis]
    return lax.dynamic_slice_in_dim(
        jnp.concatenate([values, values], axis=axis), shift, size, axis
    )


def shape(dims, dtype=BF16):
    return jax.ShapeDtypeStruct(dims, dtype)


def params(limit=10):
    return pltpu.CompilerParams(vmem_limit_bytes=limit * 1024 * 1024)


def prepare_kernel(place, strip, other, stats, by_z, by_y):
    z, y, x, core = place[0], place[1], place[2], place[3]
    for k in range(NX):
        chunk_z = lax.rem(x + k, NX)
        for source, owner in ((strip, core), (other, 1 - core)):
            for part in range(2):
                chunk_y = owner * 2 + part
                at = pl.multiple_of((chunk_z * NY + chunk_y) * CHUNK, CHUNK)
                mean = stats[pl.ds(at, CHUNK), 0:1]
                scale = stats[pl.ds(at, CHUNK), 1:2]
                values = source[k, part * CHUNK : (part + 1) * CHUNK, :].astype(F32)
                normed = ((values - mean) * scale).astype(BF16)
                away_z = lax.rem(chunk_z - z + NZ, NZ)
                away_y = lax.rem(chunk_y - y + NY, NY)
                to_z = lax.rem(away_z + 2, NZ) * NY + away_y
                to_y = lax.rem(away_y + 2, NY) * NZ + away_z
                by_z[pl.ds(pl.multiple_of(to_z * CHUNK, CHUNK), CHUNK), :] = normed
                by_y[pl.ds(pl.multiple_of(to_y * CHUNK, CHUNK), CHUNK), :] = normed


def prepare(place, strip, other, stats):
    width = strip.shape[2]
    rows = 2 * strip.shape[0] * strip.shape[1]
    return pl.pallas_call(
        prepare_kernel,
        in_specs=[pl.BlockSpec(memory_space=pltpu.SMEM), VMEM, VMEM, VMEM],
        out_specs=[VMEM] * 2,
        out_shape=[shape((rows, width))] * 2,
        compiler_params=params(),
        name="prepare",
    )(place, strip, other, stats)


def queries_kernel(place, rows, query, keyval, out):
    z, y = place[0], place[1]
    q_cols = query.shape[1]
    for weight, begin in ((query, 0), (keyval, q_cols)):
        part = dot(rows[...], weight[...]).astype(BF16)
        for k in range(NZ):
            for i in range(NY):
                chunk = lax.rem(z + k + 2, NZ) * NY + lax.rem(y + i, NY)
                at = (k * NY + i) * CHUNK
                values = part[at : at + CHUNK].reshape(CHUNK // 4, 4, weight.shape[1])
                out[pl.ds(chunk * (CHUNK // 4), CHUNK // 4), :, begin : begin + weight.shape[1]] = (
                    values
                )


def queries(place, rows, query, keyval):
    cols = query.shape[1] + keyval.shape[1]
    return pl.pallas_call(
        queries_kernel,
        in_specs=[pl.BlockSpec(memory_space=pltpu.SMEM), VMEM, VMEM, VMEM],
        out_specs=VMEM,
        out_shape=shape((rows.shape[0] // 4, 4, cols)),
        compiler_params=params(),
        name="queries",
    )(place, rows, query, keyval)


def products_kernel(rows, gate, up, later, left, right, ahead, own, behind):
    for i, weight in enumerate((gate, up)):
        out = dot(rows[...], weight[...]).astype(BF16)
        (left, right)[i][...] = out[:QUARTER]
        behind[i] = out[QUARTER : 2 * QUARTER]
        own[i] = out[2 * QUARTER : 3 * QUARTER]
        ahead[i] = out[3 * QUARTER :]


def products(rows, gate, up, begin, cols, later):
    width = rows.shape[1]
    skip = begin // BLOCK
    column = pl.BlockSpec((width, BLOCK), lambda j: (0, skip + j))
    flat = pl.BlockSpec((QUARTER, BLOCK), lambda j: (0, j))
    both = pl.BlockSpec((2, QUARTER, BLOCK), lambda j: (0, 0, j))
    return pl.pallas_call(
        products_kernel,
        grid=(cols // BLOCK,),
        in_specs=[pl.BlockSpec(rows.shape, lambda j: (0, 0)), column, column]
        + [pl.BlockSpec(memory_space=pl.ANY)],
        out_specs=[flat] * 2 + [both] * 3,
        out_shape=[shape((QUARTER, cols))] * 2 + [shape((2, QUARTER, cols))] * 3,
        compiler_params=params(56),
        name="products",
    )(rows, gate, up, later)


def second_kernel(left, right, ahead_in, behind_in, later, ahead, behind):
    ahead[0] = add(ahead_in[0], left[...]).astype(BF16)
    behind[0] = add(behind_in[0], right[...]).astype(BF16)


def second(left, right, ahead, behind, later):
    quarter, cols = left.shape
    steps = 4
    whole = pl.BlockSpec((quarter, cols // steps), lambda j: (0, j))
    first = pl.BlockSpec((1, quarter, cols // steps), lambda j: (0, 0, j))
    last = pl.BlockSpec((1, quarter, cols // steps), lambda j: (1, 0, j))
    return pl.pallas_call(
        second_kernel,
        grid=(steps,),
        in_specs=[whole, whole, first, last, pl.BlockSpec(memory_space=pl.ANY)],
        out_specs=[first, last],
        out_shape=[shape(ahead.shape)] * 2,
        input_output_aliases={2: 0, 3: 1},
        compiler_params=params(56),
        name="second",
    )(left, right, ahead, behind, later)


def total_kernel(own, left, right, later, *outs):
    for k, out in enumerate(outs):
        at = slice(k * CHUNK, (k + 1) * CHUNK)
        for i in range(2):
            out[i] = add(own[i, at, :], left[i, at, :], right[i, at, :]).astype(BF16)


def total(own, left, right, later):
    cols = own.shape[2]
    return pl.pallas_call(
        total_kernel,
        in_specs=[VMEM] * 3 + [pl.BlockSpec(memory_space=pl.ANY)],
        out_specs=[VMEM] * 4,
        out_shape=[shape((2, CHUNK, cols))] * 4,
        compiler_params=params(),
        name="total",
    )(own, left, right, later)


def hidden_kernel(own, left, right, far, *refs):
    out = refs[-1]
    gate, up = [add(own[i], left[i], right[i], far[i]) for i in range(2)]
    joined = [(gate / (1.0 + jnp.exp(-gate)) * up).astype(BF16)]
    joined = jnp.concatenate(joined + [ref[...] for ref in refs[:-1]], axis=1)
    half = out.shape[2]
    out[0] = joined[:, :half]
    out[1] = joined[:, half:]


def hidden(own, left, right, far, *att):
    cols = own.shape[2] + sum(v.shape[1] for v in att)
    return pl.pallas_call(
        hidden_kernel,
        in_specs=[VMEM] * (4 + len(att)),
        out_specs=VMEM,
        out_shape=shape((2, CHUNK, cols // 2)),
        compiler_params=params(),
        name="hidden",
    )(own, left, right, far, *att)


def attend_kernel(att, turn, keys, values, later, attended, new_kv):
    q_cols = attended.shape[3]
    count = attended.shape[0]
    heads = q_cols // HD
    half = HD // 2
    cos_part, sin_part = turn[0:1, :], turn[1:2, :]

    def rotated(v):
        first, second = v[:, :half], v[:, half:]
        return jnp.concatenate(
            [first * cos_part - second * sin_part, first * sin_part + second * cos_part], axis=1
        )

    mine = att[0].astype(F32)
    queries = jnp.concatenate([mine[:, h * HD : (h + 1) * HD] for h in range(heads)], axis=0)
    queries = (rotated(queries) * HD ** (-0.5)).astype(BF16)
    key = jnp.concatenate([mine[j : j + 1, q_cols:] for j in range(4)], axis=1)
    key = rotated(key).astype(BF16)
    value = jnp.concatenate([mine[j : j + 1, q_cols:] for j in range(4, 8)], axis=1)
    new_kv[0, :, :HD] = key
    new_kv[0, :, HD:] = value.astype(BF16)
    scores = lax.dot_general(
        queries, keys[0], (((1,), (1,)), ((), ())), preferred_element_type=F32
    )
    own = jnp.sum(queries.astype(F32) * key.astype(F32), axis=1, keepdims=True)
    top = jnp.maximum(jnp.max(scores, axis=1, keepdims=True), own)
    weights = jnp.exp(scores - top)
    own_w = jnp.exp(own - top)
    sums = jnp.sum(weights, axis=1, keepdims=True) + own_w
    probs = (weights / sums).astype(BF16)
    mixed = dot(probs, values[0]) + (own_w / sums).astype(BF16).astype(F32) * value
    for h in range(heads):
        attended[:, 0, 0, h * HD : (h + 1) * HD] = mixed[h * count : (h + 1) * count].astype(BF16)


def attend(att, q_cols, key_cache, value_cache, later):
    half = HD // 2
    freqs = 10000.0 ** (-jnp.arange(half, dtype=F32) / half)
    angles = F32(key_cache.shape[1]) * freqs
    turn = jnp.stack([jnp.cos(angles), jnp.sin(angles)])
    rows, count, cols = att.shape
    cache = pl.BlockSpec((1,) + key_cache.shape[1:], lambda r: (r, 0, 0))
    return pl.pallas_call(
        attend_kernel,
        grid=(rows,),
        in_specs=[
            pl.BlockSpec((1, count, cols), lambda r: (r, 0, 0)),
            pl.BlockSpec(turn.shape, lambda r: (0, 0)),
            cache,
            cache,
            pl.BlockSpec(memory_space=pl.ANY),
        ],
        out_specs=[
            pl.BlockSpec((count, 1, 1, q_cols), lambda r: (0, r, 0, 0)),
            pl.BlockSpec((1, 1, 2 * HD), lambda r: (r, 0, 0)),
        ],
        out_shape=[shape((count, rows, 1, q_cols)), shape((rows, 1, 2 * HD))],
        compiler_params=params(56),
        name="attend",
    )(att, turn, key_cache, value_cache, later)


def local(tokens, w_query, w_key_value, w_gate, w_up, w_attn_out, w_down, key_cache, value_cache):
    count_gx = lax.axis_size("gx")
    count_gy = lax.axis_size("gy")
    mine = lax.axis_index("gx")
    place = lax.axis_index("gy")
    z, y = mine // NY, mine % NY
    x, core = place // 2, place % 2
    width = tokens.shape[1]
    q_cols = w_query.shape[1]
    att_cols = q_cols + w_key_value.shape[1]
    hid = w_gate.shape[1]
    hid_y = hid - HID_Z
    rows_dev = CHUNK // count_gy

    values = tokens.astype(F32)
    block_mean = jnp.mean(values, axis=1)
    centered = values - block_mean[:, None]
    stats = jnp.concatenate([block_mean, jnp.sum(centered * centered, axis=1)])
    count = count_gx * count_gy
    stats = lax.all_to_all(
        jnp.broadcast_to(stats, (count, 1, stats.shape[0])), ("gx", "gy"), 0, 0
    ).reshape(count_gx, count_gy, 2, -1)
    mean = jnp.mean(stats[:, :, 0], axis=0)
    offsets = stats[:, :, 0] - mean
    spread = jnp.sum(stats[:, :, 1] + width * offsets * offsets, axis=0) / D
    stats = jnp.stack([mean.reshape(-1), lax.rsqrt(spread + 1e-05).reshape(-1)], axis=1)

    position = jnp.stack([z, y, x, core]).astype(jnp.int32)
    strip = jnp.stack(gather_direct(tokens, ring_x, "gy"))
    other = send(strip, CORES, "gy")
    by_z, by_y = prepare(position, strip, other, stats)

    att = queries(position, by_z, w_query, w_key_value)
    later = att
    att = lax.all_to_all(att, ("gx", "gy"), 0, 0)

    left_z, right_z, ahead_z, own_z, behind_z = products(by_z, w_gate, w_up, 0, HID_Z, later)
    left_y, right_y, ahead_y, own_y, behind_y = products(by_y, w_gate, w_up, HID_Z, hid_y, own_z)
    left_z = send(left_z, ring_z(1))
    right_z = send(right_z, ring_z(-1))
    left_y = send(left_y, ring_y(1))
    right_y = send(right_y, ring_y(-1))

    ahead_z, behind_z = second(left_z, right_z, ahead_z, behind_z, att)
    ahead_y, behind_y = second(left_y, right_y, ahead_y, behind_y, ahead_z)

    att = jnp.sum(att.reshape(count_gx, count_gy, rows_dev, att_cols).astype(F32), axis=0)
    att = att.astype(BF16).transpose(1, 0, 2)
    attended, new_kv = attend(att, q_cols, key_cache, value_cache, ahead_y)
    new_kv = new_kv.reshape(rows_dev, 2 * HD)
    total_z = total(own_z, send(ahead_z, ring_z(1)), send(behind_z, ring_z(-1)), attended)
    attended = lax.all_to_all(attended, "gy", 0, 0)
    total_y = total(own_y, send(ahead_y, ring_y(1)), send(behind_y, ring_y(-1)), attended)
    attended = attended.reshape(CHUNK, q_cols)

    att_z = q_cols // 2
    hidden_z = hidden(total_z[0], *send_direct(total_z, ring_y), attended[:, :att_z])
    hidden_y = hidden(total_y[0], *send_direct(total_y, ring_z), attended[:, att_z:])

    def down(part, first, second, hid, att):
        inner = jnp.concatenate(gather_direct(part, first), axis=1)
        left = send(inner, second(1))
        right = send(inner, second(-1))
        low = send(left[0], second(1))
        high = send(right[1], second(-1))
        half = part.shape[2]

        def product(low, high):
            middle = hid.stop - hid.start - half
            out = dot(low, w_down[hid.start : hid.start + half])
            out = out + dot(high[:, :middle], w_down[hid.start + half : hid.stop])
            return out + dot(high[:, middle:], w_attn_out[att])

        return jnp.concatenate(
            [
                product(inner[0], inner[1]),
                product(right[0], right[1]),
                product(low, high),
                product(left[0], left[1]),
            ],
            axis=0,
        )

    down_z = down(hidden_z, ring_y, ring_z, slice(0, HID_Z), slice(0, att_z))
    down_y = down(hidden_y, ring_z, ring_y, slice(HID_Z, hid), slice(att_z, q_cols))
    d_out = w_down.shape[1]
    terms = down_z.reshape(NZ, NY, CHUNK, d_out)
    terms = terms + down_y.reshape(NY, NZ, CHUNK, d_out).transpose(1, 0, 2, 3)
    terms = roll(roll(terms.astype(BF16), 0, (NZ - z) % NZ), 1, (NY - y) % NY)

    terms = terms.reshape(NX, 2, -1, d_out)
    theirs = lax.dynamic_index_in_dim(terms, 1 - core, 1, keepdims=False)
    ours = lax.dynamic_index_in_dim(terms, core, 1, keepdims=False)
    ours = add(ours, send(theirs, CORES, "gy")).astype(BF16)
    ours = roll(ours, 0, x)
    branch = add(ours[0], *send_direct([ours[k] for k in range(NX)], ring_x, "gy"))
    layer_out = (tokens.astype(F32) + branch).astype(BF16)
    return (layer_out, new_kv)


def solution(mesh):
    return jax.shard_map(
        local,
        mesh=mesh,
        in_specs=(
            P("gy", "gx"),
            P("gx", "gy"),
            P("gx", "gy"),
            P("gx", "gy"),
            P("gx", "gy"),
            P("gy", "gx"),
            P("gy", "gx"),
            P(("gx", "gy"), None, None),
            P(("gx", "gy"), None, None),
        ),
        out_specs=(P("gy", "gx"), P(("gx", "gy"), None)),
        check_vma=False,
    )
```

```python
import functools

import jax
import jax.numpy as jnp
from jax import lax
from jax.experimental import pallas as pl
from jax.experimental.pallas import tpu as pltpu
from jax.sharding import PartitionSpec as P

D = 8192
HEADS = 32
HD = 256
NZ = 4
NY = 4
NX = 4
CHUNK = 32
QUARTER = 128
BLOCK = 512
HID_Z = 2048
ATT = 1152
RIDE = 640
FIRST_STAT = 16
F32 = jnp.float32
BF16 = jnp.bfloat16
VMEM = pl.BlockSpec(memory_space=pltpu.VMEM)


def ring_y(shift):
    return [(z * NY + y, z * NY + (y + shift) % NY) for z in range(NZ) for y in range(NY)]


def ring_z(shift):
    return [(z * NY + y, ((z + shift) % NZ) * NY + y) for z in range(NZ) for y in range(NY)]


def ring_x(shift):
    return [(x * 2 + c, ((x + shift) % NX) * 2 + c) for x in range(NX) for c in range(2)]


CORES = [(x * 2 + c, x * 2 + 1 - c) for x in range(NX) for c in range(2)]


def send(value, pairs, axis="gx"):
    return lax.ppermute(value, axis, pairs)


def send_direct(chunks, ring, axis="gx"):
    return (
        send(chunks[1], ring(1), axis),
        send(chunks[3], ring(-1), axis),
        send(chunks[2], ring(2), axis),
    )


def gather_direct(value, ring, axis="gx"):
    left, right, far = send_direct([value] * 4, ring, axis)
    return [value, right, far, left]


def add(*values):
    total = values[0].astype(F32)
    for value in values[1:]:
        total = total + value.astype(F32)
    return total


def dot(a, b):
    return jnp.dot(a, b, preferred_element_type=F32)


def roll(values, axis, shift):
    size = values.shape[axis]
    return lax.dynamic_slice_in_dim(
        jnp.concatenate([values, values], axis=axis), shift, size, axis
    )


def shape(dims, dtype=BF16):
    return jax.ShapeDtypeStruct(dims, dtype)


def params(limit=10):
    return pltpu.CompilerParams(vmem_limit_bytes=limit * 1024 * 1024)


def prepare_kernel(place, strip, other, by_z, by_y, stats):
    z, y, x, core = place[0], place[1], place[2], place[3]
    stats[...] = jnp.zeros(stats.shape, BF16)
    for k in range(NX):
        chunk_z = lax.rem(x + k, NX)
        for source, owner in ((strip, core), (other, 1 - core)):
            for part in range(2):
                chunk_y = owner * 2 + part
                values = source[k, part * CHUNK : (part + 1) * CHUNK, :].astype(F32)
                mean = jnp.mean(values, axis=1, keepdims=True)
                centered = values - mean
                spread = jnp.sum(centered * centered, axis=1, keepdims=True)
                centered = centered.astype(BF16)
                away_z = lax.rem(chunk_z - z + NZ, NZ)
                away_y = lax.rem(chunk_y - y + NY, NY)
                to_z = lax.rem(away_z + 2, NZ) * NY + away_y
                to_y = lax.rem(away_y + 2, NY) * NZ + away_z
                by_z[pl.ds(pl.multiple_of(to_z * CHUNK, CHUNK), CHUNK), :] = centered
                by_y[pl.ds(pl.multiple_of(to_y * CHUNK, CHUNK), CHUNK), :] = centered
                lane = lax.broadcasted_iota(jnp.int32, (CHUNK, 128), 1)
                parts = jnp.zeros((CHUNK, 128), F32)
                for i, value in enumerate((mean, spread)):
                    for n in range(3):
                        piece = value.astype(BF16).astype(F32)
                        parts = jnp.where(lane == FIRST_STAT + 3 * i + n, piece, parts)
                        value = value - piece
                at = (chunk_z * NY + chunk_y) * (CHUNK // 4)
                stats[pl.ds(at, CHUNK // 4), :, RIDE - 128 :] = parts.astype(BF16).reshape(
                    CHUNK // 4, 4, 128
                )


def prepare(place, strip, other):
    width = strip.shape[2]
    rows = 2 * strip.shape[0] * strip.shape[1]
    return pl.pallas_call(
        prepare_kernel,
        in_specs=[pl.BlockSpec(memory_space=pltpu.SMEM), VMEM, VMEM],
        out_specs=[VMEM] * 3,
        out_shape=[shape((rows, width))] * 2 + [shape((rows // 4, 4, RIDE))],
        compiler_params=params(),
        name="prepare",
    )(place, strip, other)


def queries_kernel(place, rows, query, keyval, riders, stats, out):
    z, y = place[0], place[1]
    q_cols = query.shape[1]
    out[:, :, q_cols:ATT] = jnp.zeros((out.shape[0], 4, ATT - q_cols), BF16)
    for weight, begin in ((query, 0), (keyval, q_cols)):
        part = dot(rows[...], weight[...]).astype(BF16)
        for k in range(NZ):
            for i in range(NY):
                chunk = lax.rem(z + k + 2, NZ) * NY + lax.rem(y + i, NY)
                at = (k * NY + i) * CHUNK
                values = part[at : at + CHUNK].reshape(CHUNK // 4, 4, weight.shape[1])
                out[pl.ds(chunk * (CHUNK // 4), CHUNK // 4), :, begin : begin + weight.shape[1]] = (
                    values
                )
    for n in range(0, out.shape[0], riders.shape[0]):
        at = slice(n, n + riders.shape[0])
        out[at, :, ATT:] = riders[...] + stats[at]


def queries(place, rows, query, keyval, riders, stats):
    return pl.pallas_call(
        queries_kernel,
        in_specs=[pl.BlockSpec(memory_space=pltpu.SMEM)] + [VMEM] * 5,
        out_specs=VMEM,
        out_shape=shape((rows.shape[0] // 4, 4, ATT + RIDE)),
        compiler_params=params(16),
        name="queries",
    )(place, rows, query, keyval, riders, stats)


def products_kernel(rows, gate, up, later, left, right, ahead, own, behind):
    for i, weight in enumerate((gate, up)):
        out = dot(rows[...], weight[...]).astype(BF16)
        (left, right)[i][...] = out[:QUARTER]
        behind[i] = out[QUARTER : 2 * QUARTER]
        own[i] = out[2 * QUARTER : 3 * QUARTER]
        ahead[i] = out[3 * QUARTER :]


def products(rows, gate, up, begin, cols, later):
    width = rows.shape[1]
    skip = begin // BLOCK
    column = pl.BlockSpec((width, BLOCK), lambda j: (0, skip + j))
    flat = pl.BlockSpec((QUARTER, BLOCK), lambda j: (0, j))
    both = pl.BlockSpec((2, QUARTER, BLOCK), lambda j: (0, 0, j))
    return pl.pallas_call(
        products_kernel,
        grid=(cols // BLOCK,),
        in_specs=[pl.BlockSpec(rows.shape, lambda j: (0, 0)), column, column]
        + [pl.BlockSpec(memory_space=pl.ANY)],
        out_specs=[flat] * 2 + [both] * 3,
        out_shape=[shape((QUARTER, cols))] * 2 + [shape((2, QUARTER, cols))] * 3,
        compiler_params=params(56),
        name="products",
    )(rows, gate, up, later)


def second_kernel(left, right, ahead_in, behind_in, later, ahead, behind):
    ahead[0] = add(ahead_in[0], left[...]).astype(BF16)
    behind[0] = add(behind_in[0], right[...]).astype(BF16)


def second(left, right, ahead, behind, later):
    whole = pl.BlockSpec(left.shape, lambda j: (0, 0))
    first = pl.BlockSpec((1,) + left.shape, lambda j: (0, 0, 0))
    last = pl.BlockSpec((1,) + left.shape, lambda j: (1, 0, 0))
    return pl.pallas_call(
        second_kernel,
        grid=(1,),
        in_specs=[whole, whole, first, last, pl.BlockSpec(memory_space=pl.ANY)],
        out_specs=[first, last],
        out_shape=[shape(ahead.shape)] * 2,
        input_output_aliases={2: 0, 3: 1},
        compiler_params=params(56),
        name="second",
    )(left, right, ahead, behind, later)


def total_kernel(own, left, right, later, *outs):
    for k, out in enumerate(outs):
        at = slice(k * CHUNK, (k + 1) * CHUNK)
        for i in range(2):
            out[i] = add(own[i, at, :], left[i, at, :], right[i, at, :]).astype(BF16)


def total(own, left, right, later):
    cols = own.shape[2]
    return pl.pallas_call(
        total_kernel,
        in_specs=[VMEM] * 3 + [pl.BlockSpec(memory_space=pl.ANY)],
        out_specs=[VMEM] * 4,
        out_shape=[shape((2, CHUNK, cols))] * 4,
        compiler_params=params(),
        name="total",
    )(own, left, right, later)


def hidden_kernel(own, left, right, far, offsets, sums, scale, *refs):
    out = refs[-1]
    both = []
    for i in range(2):
        value = add(own[i], left[i], right[i], far[i]) + dot(offsets[...], sums[i])
        both.append(value * scale[...])
    gate, up = both
    joined = [(gate / (1.0 + jnp.exp(-gate)) * up).astype(BF16)]
    joined = jnp.concatenate(joined + [ref[...] for ref in refs[:-1]], axis=1)
    half = out.shape[2]
    out[0] = joined[:, :half]
    out[1] = joined[:, half:]


def hidden(own, left, right, far, offsets, sums, scale, *att):
    cols = own.shape[2] + sum(v.shape[1] for v in att)
    return pl.pallas_call(
        hidden_kernel,
        in_specs=[VMEM] * (7 + len(att)),
        out_specs=VMEM,
        out_shape=shape((2, CHUNK, cols // 2)),
        compiler_params=params(),
        name="hidden",
    )(own, left, right, far, offsets, sums, scale, *att)


def attend_kernel(att, turn, keys, values, later, attended, new_kv):
    q_cols = attended.shape[3]
    count = attended.shape[0]
    heads = q_cols // HD
    half = HD // 2
    cos_part, sin_part = turn[0:1, :], turn[1:2, :]

    def rotated(v):
        first, second = v[:, :half], v[:, half:]
        return jnp.concatenate(
            [first * cos_part - second * sin_part, first * sin_part + second * cos_part], axis=1
        )

    mine = att[0].astype(F32)
    queries = jnp.concatenate([mine[:, h * HD : (h + 1) * HD] for h in range(heads)], axis=0)
    queries = (rotated(queries) * HD ** (-0.5)).astype(BF16)
    key = jnp.concatenate([mine[j : j + 1, q_cols:] for j in range(4)], axis=1)
    key = rotated(key).astype(BF16)
    value = jnp.concatenate([mine[j : j + 1, q_cols:] for j in range(4, 8)], axis=1)
    new_kv[0, :, :HD] = key
    new_kv[0, :, HD:] = value.astype(BF16)
    scores = lax.dot_general(
        queries, keys[0], (((1,), (1,)), ((), ())), preferred_element_type=F32
    )
    own = jnp.sum(queries.astype(F32) * key.astype(F32), axis=1, keepdims=True)
    top = jnp.maximum(jnp.max(scores, axis=1, keepdims=True), own)
    weights = jnp.exp(scores - top)
    own_w = jnp.exp(own - top)
    sums = jnp.sum(weights, axis=1, keepdims=True) + own_w
    probs = (weights / sums).astype(BF16)
    mixed = dot(probs, values[0]) + (own_w / sums).astype(BF16).astype(F32) * value
    for h in range(heads):
        attended[:, 0, 0, h * HD : (h + 1) * HD] = mixed[h * count : (h + 1) * count].astype(BF16)


def attend(att, q_cols, key_cache, value_cache, later):
    half = HD // 2
    freqs = 10000.0 ** (-jnp.arange(half, dtype=F32) / half)
    angles = F32(key_cache.shape[1]) * freqs
    turn = jnp.stack([jnp.cos(angles), jnp.sin(angles)])
    rows, count, cols = att.shape
    cache = pl.BlockSpec((1,) + key_cache.shape[1:], lambda r: (r, 0, 0))
    return pl.pallas_call(
        attend_kernel,
        grid=(rows,),
        in_specs=[
            pl.BlockSpec((1, count, cols), lambda r: (r, 0, 0)),
            pl.BlockSpec(turn.shape, lambda r: (0, 0)),
            cache,
            cache,
            pl.BlockSpec(memory_space=pl.ANY),
        ],
        out_specs=[
            pl.BlockSpec((count, 1, 1, q_cols), lambda r: (0, r, 0, 0)),
            pl.BlockSpec((1, 1, 2 * HD), lambda r: (r, 0, 0)),
        ],
        out_shape=[shape((count, rows, 1, q_cols)), shape((rows, 1, 2 * HD))],
        compiler_params=params(56),
        name="attend",
    )(att, turn, key_cache, value_cache, later)


def local(tokens, w_query, w_key_value, w_gate, w_up, w_attn_out, w_down, key_cache, value_cache):
    count_gx = lax.axis_size("gx")
    count_gy = lax.axis_size("gy")
    mine = lax.axis_index("gx")
    place = lax.axis_index("gy")
    z, y = mine // NY, mine % NY
    x, core = place // 2, place % 2
    width = tokens.shape[1]
    q_cols = w_query.shape[1]
    att_cols = q_cols + w_key_value.shape[1]
    hid = w_gate.shape[1]
    hid_y = hid - HID_Z
    rows_dev = CHUNK // count_gy

    ones = jnp.ones((8, width), BF16)
    sums = [dot(ones, w)[:1].astype(BF16) for w in (w_query, w_key_value, w_gate, w_up)]
    sums_att = jnp.concatenate(sums[:2], axis=1).reshape(1, 4, -1)
    sums_hid = jnp.concatenate(sums[2:], axis=1).reshape(count_gy, 4, -1)
    sums_att = jnp.broadcast_to(sums_att, (count_gy,) + sums_att.shape[1:])
    riders = jnp.concatenate([sums_att, sums_hid], axis=2)
    ride = riders.shape[2]
    riders = jnp.pad(riders, ((0, 0), (0, 0), (0, RIDE - ride)))

    position = jnp.stack([z, y, x, core]).astype(jnp.int32)
    strip = jnp.stack(gather_direct(tokens, ring_x, "gy"))
    other = send(strip, CORES, "gy")
    by_z, by_y, stats = prepare(position, strip, other)

    att = queries(position, by_z, w_query, w_key_value, riders, stats)
    later = att
    att = lax.all_to_all(att, ("gx", "gy"), 0, 0)

    left_z, right_z, ahead_z, own_z, behind_z = products(by_z, w_gate, w_up, 0, HID_Z, later)
    left_y, right_y, ahead_y, own_y, behind_y = products(by_y, w_gate, w_up, HID_Z, hid_y, own_z)
    left_z = send(left_z, ring_z(1))
    right_z = send(right_z, ring_z(-1))
    left_y = send(left_y, ring_y(1))
    right_y = send(right_y, ring_y(-1))

    ahead_z, behind_z = second(left_z, right_z, ahead_z, behind_z, att)
    ahead_y, behind_y = second(left_y, right_y, ahead_y, behind_y, ahead_z)

    att = att.reshape(count_gx, count_gy, rows_dev, ATT + RIDE)
    quarter = att_cols // 4
    stats = att[:, 0, :, ATT + ride : ATT + ride + 6].astype(F32)
    means = stats[:, :, 0] + stats[:, :, 1] + stats[:, :, 2]
    spread = stats[:, :, 3] + stats[:, :, 4] + stats[:, :, 5]
    offsets = means - jnp.mean(means, axis=0)
    spread = jnp.sum(spread + width * offsets * offsets, axis=0) / D
    scale = lax.rsqrt(spread + 1e-05)
    offsets = offsets.astype(BF16)
    sums_att = att[:, :, :, ATT : ATT + quarter].reshape(count_gx, count_gy, att_cols)
    sums_hid = att[:, :, :, ATT + quarter : ATT + ride].reshape(count_gx, count_gy, q_cols)
    high = scale.astype(BF16)
    rest = scale - high.astype(F32)
    middle = rest.astype(BF16)
    low = (rest - middle.astype(F32)).astype(BF16)
    extra = jnp.concatenate([offsets.reshape(-1), high, middle, low])
    n_off = offsets.size
    extra = jnp.pad(extra, (0, q_cols - extra.size)).reshape(1, 1, q_cols)
    extra = jnp.broadcast_to(extra, (count_gy, 8 - rows_dev, q_cols))

    att = jnp.sum(att[:, :, :, :att_cols].astype(F32), axis=0) + jnp.einsum(
        "br,bjc->jrc", offsets, sums_att, preferred_element_type=F32
    )
    att = (att * scale[:, None]).astype(BF16).transpose(1, 0, 2)
    ahead_y = send(ahead_y, ring_y(1))
    behind_y = send(behind_y, ring_y(-1))
    attended, new_kv = attend(att, q_cols, key_cache, value_cache, later)
    new_kv = new_kv.reshape(rows_dev, 2 * HD)
    back = jnp.concatenate(
        [attended.reshape(count_gy, rows_dev, q_cols), extra, sums_hid.transpose(1, 0, 2)], axis=1
    )
    back = lax.all_to_all(back, "gy", 0, 0)
    total_z = total(own_z, send(ahead_z, ring_z(1)), send(behind_z, ring_z(-1)), back)
    total_y = total(own_y, ahead_y, behind_y, back)
    attended = back[:, :rows_dev].reshape(CHUNK, q_cols)
    extra = back[:, rows_dev]
    sums_hid = back[:, 8:].transpose(1, 0, 2).reshape(count_gx, -1)
    offsets = extra[:, :n_off].reshape(count_gy, count_gx, rows_dev).transpose(0, 2, 1)
    offsets = offsets.reshape(CHUNK, count_gx)
    scale = extra[:, n_off : n_off + 3 * rows_dev].reshape(count_gy, 3, rows_dev)
    scale = add(scale[:, 0], scale[:, 1], scale[:, 2]).reshape(CHUNK, 1)

    att_z = q_cols // 2

    def column_sums(begin, end):
        return jnp.stack([sums_hid[:, begin:end], sums_hid[:, hid + begin : hid + end]])

    hidden_z = hidden(
        total_z[0], *send_direct(total_z, ring_y), offsets, column_sums(0, HID_Z), scale,
        attended[:, :att_z],
    )
    hidden_y = hidden(
        total_y[0], *send_direct(total_y, ring_z), offsets, column_sums(HID_Z, hid), scale,
        attended[:, att_z:],
    )

    def down(part, first, second, hid, att):
        inner = jnp.concatenate(gather_direct(part, first), axis=1)
        left = send(inner, second(1))
        right = send(inner, second(-1))
        low = send(left[0], second(1))
        high = send(right[1], second(-1))
        half = part.shape[2]

        def product(low, high):
            middle = hid.stop - hid.start - half
            out = dot(low, w_down[hid.start : hid.start + half])
            out = out + dot(high[:, :middle], w_down[hid.start + half : hid.stop])
            return out + dot(high[:, middle:], w_attn_out[att])

        return jnp.concatenate(
            [
                product(inner[0], inner[1]),
                product(right[0], right[1]),
                product(low, high),
                product(left[0], left[1]),
            ],
            axis=0,
        )

    down_z = down(hidden_z, ring_y, ring_z, slice(0, HID_Z), slice(0, att_z))
    down_y = down(hidden_y, ring_z, ring_y, slice(HID_Z, hid), slice(att_z, q_cols))
    d_out = w_down.shape[1]
    terms = down_z.reshape(NZ, NY, CHUNK, d_out)
    terms = terms + down_y.reshape(NY, NZ, CHUNK, d_out).transpose(1, 0, 2, 3)
    terms = roll(roll(terms.astype(BF16), 0, (NZ - z) % NZ), 1, (NY - y) % NY)

    terms = terms.reshape(NX, 2, -1, d_out)
    theirs = lax.dynamic_index_in_dim(terms, 1 - core, 1, keepdims=False)
    ours = lax.dynamic_index_in_dim(terms, core, 1, keepdims=False)
    ours = add(ours, send(theirs, CORES, "gy")).astype(BF16)
    ours = roll(ours, 0, x)
    branch = add(ours[0], *send_direct([ours[k] for k in range(NX)], ring_x, "gy"))
    layer_out = (tokens.astype(F32) + branch).astype(BF16)
    return (layer_out, new_kv)


def solution(mesh):
    return jax.shard_map(
        local,
        mesh=mesh,
        in_specs=(
            P("gy", "gx"),
            P("gx", "gy"),
            P("gx", "gy"),
            P("gx", "gy"),
            P("gx", "gy"),
            P("gy", "gx"),
            P("gy", "gx"),
            P(("gx", "gy"), None, None),
            P(("gx", "gy"), None, None),
        ),
        out_specs=(P("gy", "gx"), P(("gx", "gy"), None)),
        check_vma=False,
    )
```

```python
import functools

import jax
import jax.numpy as jnp
from jax import lax
from jax.experimental import pallas as pl
from jax.experimental.pallas import tpu as pltpu
from jax.sharding import PartitionSpec as P

D = 8192
HEADS = 32
HD = 256
NZ = 4
NY = 4
NX = 4
CHUNK = 32
QUARTER = 128
BLOCK = 512
HID_Z = 2048
ATT = 1152
FIRST_STAT = 64
SUMS_ATT = 384
SUMS_HID = 256
RIDE = SUMS_ATT + SUMS_HID
F32 = jnp.float32
BF16 = jnp.bfloat16
VMEM = pl.BlockSpec(memory_space=pltpu.VMEM)


def ring_y(shift):
    return [(z * NY + y, z * NY + (y + shift) % NY) for z in range(NZ) for y in range(NY)]


def ring_z(shift):
    return [(z * NY + y, ((z + shift) % NZ) * NY + y) for z in range(NZ) for y in range(NY)]


def ring_x(shift):
    return [(x * 2 + c, ((x + shift) % NX) * 2 + c) for x in range(NX) for c in range(2)]


CORES = [(x * 2 + c, x * 2 + 1 - c) for x in range(NX) for c in range(2)]


def send(value, pairs, axis="gx"):
    return lax.ppermute(value, axis, pairs)


def send_direct(chunks, ring, axis="gx"):
    return (
        send(chunks[1], ring(1), axis),
        send(chunks[3], ring(-1), axis),
        send(chunks[2], ring(2), axis),
    )


def gather_direct(value, ring, axis="gx"):
    left, right, far = send_direct([value] * 4, ring, axis)
    return [value, right, far, left]


def add(*values):
    total = values[0].astype(F32)
    for value in values[1:]:
        total = total + value.astype(F32)
    return total


def dot(a, b):
    return jnp.dot(a, b, preferred_element_type=F32)


def roll(values, axis, shift):
    size = values.shape[axis]
    return lax.dynamic_slice_in_dim(
        jnp.concatenate([values, values], axis=axis), shift, size, axis
    )


def shape(dims, dtype=BF16):
    return jax.ShapeDtypeStruct(dims, dtype)


def params(limit=10):
    return pltpu.CompilerParams(vmem_limit_bytes=limit * 1024 * 1024)


def prepare_kernel(place, strip, other, by_z, by_y, stats):
    z, y, x, core = place[0], place[1], place[2], place[3]
    for k in range(NX):
        chunk_z = lax.rem(x + k, NX)
        for source, owner in ((strip, core), (other, 1 - core)):
            for part in range(2):
                chunk_y = owner * 2 + part
                values = source[k, part * CHUNK : (part + 1) * CHUNK, :].astype(F32)
                mean = jnp.mean(values, axis=1, keepdims=True)
                centered = values - mean
                spread = jnp.sum(centered * centered, axis=1, keepdims=True)
                centered = centered.astype(BF16)
                away_z = lax.rem(chunk_z - z + NZ, NZ)
                away_y = lax.rem(chunk_y - y + NY, NY)
                to_z = lax.rem(away_z + 2, NZ) * NY + away_y
                to_y = lax.rem(away_y + 2, NY) * NZ + away_z
                by_z[pl.ds(pl.multiple_of(to_z * CHUNK, CHUNK), CHUNK), :] = centered
                by_y[pl.ds(pl.multiple_of(to_y * CHUNK, CHUNK), CHUNK), :] = centered
                lane = lax.broadcasted_iota(jnp.int32, (CHUNK, 128), 1)
                parts = jnp.zeros((CHUNK, 128), F32)
                for i, value in enumerate((mean, spread)):
                    for n in range(3):
                        piece = value.astype(BF16).astype(F32)
                        parts = jnp.where(lane == FIRST_STAT + 3 * i + n, piece, parts)
                        value = value - piece
                at = (chunk_z * NY + chunk_y) * (CHUNK // 4)
                stats[pl.ds(at, CHUNK // 4), :, :] = parts.astype(BF16).reshape(
                    CHUNK // 4, 4, 128
                )


def prepare(place, strip, other):
    width = strip.shape[2]
    rows = 2 * strip.shape[0] * strip.shape[1]
    return pl.pallas_call(
        prepare_kernel,
        in_specs=[pl.BlockSpec(memory_space=pltpu.SMEM), VMEM, VMEM],
        out_specs=[VMEM] * 3,
        out_shape=[shape((rows, width))] * 2 + [shape((rows // 4, 4, 128))],
        compiler_params=params(),
        name="prepare",
    )(place, strip, other)


def queries_kernel(place, rows, query, keyval, riders, stats, out):
    z, y = place[0], place[1]
    q_cols = query.shape[1]
    out[:, :, ATT - 128 : ATT] = stats[...]
    for weight, begin in ((query, 0), (keyval, q_cols)):
        part = dot(rows[...], weight[...]).astype(BF16)
        for k in range(NZ):
            for i in range(NY):
                chunk = lax.rem(z + k + 2, NZ) * NY + lax.rem(y + i, NY)
                at = (k * NY + i) * CHUNK
                values = part[at : at + CHUNK].reshape(CHUNK // 4, 4, weight.shape[1])
                out[pl.ds(chunk * (CHUNK // 4), CHUNK // 4), :, begin : begin + weight.shape[1]] = (
                    values
                )
    for n in range(0, out.shape[0], riders.shape[0]):
        at = slice(n, n + riders.shape[0])
        out[at, :, ATT:] = riders[...]


def queries(place, rows, query, keyval, riders, stats):
    return pl.pallas_call(
        queries_kernel,
        in_specs=[pl.BlockSpec(memory_space=pltpu.SMEM)] + [VMEM] * 5,
        out_specs=VMEM,
        out_shape=shape((rows.shape[0] // 4, 4, ATT + RIDE)),
        compiler_params=params(16),
        name="queries",
    )(place, rows, query, keyval, riders, stats)


def products_kernel(rows, gate, up, later, ahead, behind, gate_on, up_on, own):
    for i, weight in enumerate((gate, up)):
        out = dot(rows[...], weight[...]).astype(BF16)
        (ahead, behind)[i][i] = out[:QUARTER]
        own[i] = out[2 * QUARTER : 3 * QUARTER]
        if i == 0:
            behind[0] = out[QUARTER : 2 * QUARTER]
            gate_on[...] = out[3 * QUARTER :]
        else:
            up_on[...] = out[QUARTER : 2 * QUARTER]
            ahead[1] = out[3 * QUARTER :]


def products(rows, gate, up, begin, cols, later):
    width = rows.shape[1]
    skip = begin // BLOCK
    column = pl.BlockSpec((width, BLOCK), lambda j: (0, skip + j))
    flat = pl.BlockSpec((QUARTER, BLOCK), lambda j: (0, j))
    both = pl.BlockSpec((2, QUARTER, BLOCK), lambda j: (0, 0, j))
    return pl.pallas_call(
        products_kernel,
        grid=(cols // BLOCK,),
        in_specs=[pl.BlockSpec(rows.shape, lambda j: (0, 0)), column, column]
        + [pl.BlockSpec(memory_space=pl.ANY)],
        out_specs=[both] * 2 + [flat] * 2 + [both],
        out_shape=[shape((2, QUARTER, cols))] * 2
        + [shape((QUARTER, cols))] * 2
        + [shape((2, QUARTER, cols))],
        compiler_params=params(56),
        name="products",
    )(rows, gate, up, later)


def second_kernel(left, right, gate_in, up_in, later, gate, up):
    gate[...] = add(gate_in[...], left[0]).astype(BF16)
    up[...] = add(up_in[...], right[0]).astype(BF16)


def half(values, i):
    return pl.BlockSpec((1,) + values.shape[1:], lambda j: (i, 0, 0))


def whole(values):
    return pl.BlockSpec(values.shape, lambda j: (0,) * values.ndim)


def second(left, right, gate, up, later):
    return pl.pallas_call(
        second_kernel,
        grid=(1,),
        in_specs=[half(left, 0), half(right, 1), whole(gate), whole(up)]
        + [pl.BlockSpec(memory_space=pl.ANY)],
        out_specs=[whole(gate), whole(up)],
        out_shape=[shape(gate.shape)] * 2,
        compiler_params=params(10),
        name="second",
    )(left, right, gate, up, later)


def total_kernel(own, left, right, gate, up, later, *outs):
    for k, out in enumerate(outs):
        at = slice(k * CHUNK, (k + 1) * CHUNK)
        out[0] = add(own[0, at, :], gate[at, :], right[0, at, :]).astype(BF16)
        out[1] = add(own[1, at, :], left[0, at, :], up[at, :]).astype(BF16)


def total(own, left, right, gate, up, later):
    outs = [shape((2, CHUNK, own.shape[2]))] * 4
    return pl.pallas_call(
        total_kernel,
        grid=(1,),
        in_specs=[whole(own), half(left, 1), half(right, 0), whole(gate), whole(up)]
        + [pl.BlockSpec(memory_space=pl.ANY)],
        out_specs=[whole(out) for out in outs],
        out_shape=outs,
        compiler_params=params(),
        name="total",
    )(own, left, right, gate, up, later)


def hidden_kernel(own, left, right, far, offsets, sums, scale, *refs):
    out = refs[-1]
    both = []
    for i in range(2):
        value = add(own[i], left[i], right[i], far[i]) + dot(offsets[...], sums[i])
        both.append(value * scale[...])
    gate, up = both
    joined = [(gate / (1.0 + jnp.exp(-gate)) * up).astype(BF16)]
    joined = jnp.concatenate(joined + [ref[...] for ref in refs[:-1]], axis=1)
    half = out.shape[2]
    out[0] = joined[:, :half]
    out[1] = joined[:, half:]


def hidden(own, left, right, far, offsets, sums, scale, *att):
    cols = own.shape[2] + sum(v.shape[1] for v in att)
    return pl.pallas_call(
        hidden_kernel,
        in_specs=[VMEM] * (7 + len(att)),
        out_specs=VMEM,
        out_shape=shape((2, CHUNK, cols // 2)),
        compiler_params=params(),
        name="hidden",
    )(own, left, right, far, offsets, sums, scale, *att)


def attend_kernel(come, turn, keys, values, later, back, new_kv, att, attended, *, width, q_cols):
    row = pl.program_id(0)
    blocks = come.shape[0] // back.shape[0]
    count = back.shape[0]
    rows = att.shape[0]
    heads = q_cols // HD
    half = HD // 2

    @pl.when(row == 0)
    def _():
        means, spreads = [], []
        for b in range(blocks):
            stats = come[b * count, :, ATT - 128 : ATT].astype(F32)
            at = [stats[:, FIRST_STAT + i : FIRST_STAT + i + 1] for i in range(6)]
            means.append(at[0] + at[1] + at[2])
            spreads.append(at[3] + at[4] + at[5])
        mean = sum(means[1:], means[0]) / blocks
        offsets = [value - mean for value in means]
        spread = sum(v + width * o * o for v, o in zip(spreads, offsets)) / D
        scale = lax.rsqrt(spread + 1e-05)
        total = jnp.zeros((count, rows, ATT), F32)
        for b in range(blocks):
            at = slice(b * count, (b + 1) * count)
            sums = jnp.concatenate(
                [come[at, i : i + 1, ATT : ATT + SUMS_ATT] for i in range(ATT // SUMS_ATT)], axis=2
            )
            total = total + come[at, :, :ATT].astype(F32) + offsets[b][None] * sums.astype(F32)
            back[:, 8 + b : 9 + b, :] = jnp.concatenate(
                [come[at, i : i + 1, ATT + SUMS_ATT :] for i in range(rows)], axis=2
            )
        total = (total * scale[None]).astype(BF16)
        for r in range(rows):
            att[r] = total[:, r, :]
        lane = lax.broadcasted_iota(jnp.int32, (rows, back.shape[2]), 1)
        line = lax.broadcasted_iota(jnp.int32, (rows, back.shape[2]), 0)
        pieces = list(offsets)
        rest = scale
        for _ in range(3):
            pieces.append(rest.astype(BF16).astype(F32))
            rest = rest - pieces[-1]
        extra = jnp.zeros(lane.shape, F32)
        for i, piece in enumerate(pieces):
            extra = extra + jnp.where(lane == i * rows + line, piece, 0.0)
        extra = jnp.sum(extra, axis=0, keepdims=True).astype(BF16)
        back[:, rows:8, :] = jnp.broadcast_to(extra[None], (count, 8 - rows, back.shape[2]))

    cos_part, sin_part = turn[0:1, :], turn[1:2, :]

    def rotated(v):
        first, second = v[:, :half], v[:, half:]
        return jnp.concatenate(
            [first * cos_part - second * sin_part, first * sin_part + second * cos_part], axis=1
        )

    mine = att[row].astype(F32)
    queries = jnp.concatenate([mine[:, h * HD : (h + 1) * HD] for h in range(heads)], axis=0)
    queries = (rotated(queries) * HD ** (-0.5)).astype(BF16)
    part = 2 * HD // count
    key = jnp.concatenate([mine[j : j + 1, q_cols : q_cols + part] for j in range(4)], axis=1)
    key = rotated(key).astype(BF16)
    value = jnp.concatenate([mine[j : j + 1, q_cols : q_cols + part] for j in range(4, 8)], axis=1)
    new_kv[0, :, :HD] = key
    new_kv[0, :, HD:] = value.astype(BF16)
    scores = lax.dot_general(
        queries, keys[0], (((1,), (1,)), ((), ())), preferred_element_type=F32
    )
    own = jnp.sum(queries.astype(F32) * key.astype(F32), axis=1, keepdims=True)
    top = jnp.maximum(jnp.max(scores, axis=1, keepdims=True), own)
    weights = jnp.exp(scores - top)
    own_w = jnp.exp(own - top)
    sums = jnp.sum(weights, axis=1, keepdims=True) + own_w
    probs = (weights / sums).astype(BF16)
    mixed = dot(probs, values[0]) + (own_w / sums).astype(BF16).astype(F32) * value
    for h in range(heads):
        attended[row, :, h * HD : (h + 1) * HD] = mixed[h * count : (h + 1) * count].astype(BF16)

    @pl.when(row == rows - 1)
    def _():
        for r in range(rows):
            back[:, r, :] = attended[r]


def attend(come, count, width, q_cols, key_cache, value_cache, later):
    half = HD // 2
    freqs = 10000.0 ** (-jnp.arange(half, dtype=F32) / half)
    angles = F32(key_cache.shape[1]) * freqs
    turn = jnp.stack([jnp.cos(angles), jnp.sin(angles)])
    rows = come.shape[1]
    blocks = come.shape[0] // count
    cache = pl.BlockSpec((1,) + key_cache.shape[1:], lambda r: (r, 0, 0))
    back = shape((count, 8 + blocks, q_cols))
    return pl.pallas_call(
        functools.partial(attend_kernel, width=width, q_cols=q_cols),
        grid=(rows,),
        in_specs=[whole(come), whole(turn), cache, cache, pl.BlockSpec(memory_space=pl.ANY)],
        out_specs=[whole(back), pl.BlockSpec((1, 1, 2 * HD), lambda r: (r, 0, 0))],
        out_shape=[back, shape((rows, 1, 2 * HD))],
        scratch_shapes=[
            pltpu.VMEM((rows, count, ATT), BF16),
            pltpu.VMEM((rows, count, q_cols), BF16),
        ],
        compiler_params=params(16),
        name="attend",
    )(come, turn, key_cache, value_cache, later)


def local(tokens, w_query, w_key_value, w_gate, w_up, w_attn_out, w_down, key_cache, value_cache):
    count_gx = lax.axis_size("gx")
    count_gy = lax.axis_size("gy")
    mine = lax.axis_index("gx")
    place = lax.axis_index("gy")
    z, y = mine // NY, mine % NY
    x, core = place // 2, place % 2
    width = tokens.shape[1]
    q_cols = w_query.shape[1]
    att_cols = q_cols + w_key_value.shape[1]
    hid = w_gate.shape[1]
    hid_y = hid - HID_Z
    rows_dev = CHUNK // count_gy

    ones = jnp.ones((8, width), BF16)
    sums = [dot(ones, w)[:1].astype(BF16) for w in (w_query, w_key_value, w_gate, w_up)]
    sums_att = jnp.pad(jnp.concatenate(sums[:2], axis=1), ((0, 0), (0, 4 * SUMS_ATT - att_cols)))
    sums_att = jnp.broadcast_to(sums_att.reshape(1, 4, SUMS_ATT), (count_gy, 4, SUMS_ATT))
    sums_hid = jnp.concatenate(sums[2:], axis=1).reshape(count_gy, 4, SUMS_HID)
    riders = jnp.concatenate([sums_att, sums_hid], axis=2)

    position = jnp.stack([z, y, x, core]).astype(jnp.int32)
    strip = jnp.stack(gather_direct(tokens, ring_x, "gy"))
    other = send(strip, CORES, "gy")
    by_z, by_y, stats = prepare(position, strip, other)

    att = queries(position, by_z, w_query, w_key_value, riders, stats)
    later = att
    att = lax.all_to_all(att, ("gx", "gy"), 0, 0)

    ahead_z, behind_z, gate_z, up_z, own_z = products(by_z, w_gate, w_up, 0, HID_Z, later)
    ahead_y, behind_y, gate_y, up_y, own_y = products(by_y, w_gate, w_up, HID_Z, hid_y, own_z)
    left_z = send(ahead_z, ring_z(1))
    right_z = send(behind_z, ring_z(-1))
    left_y = send(ahead_y, ring_y(1))
    right_y = send(behind_y, ring_y(-1))

    back, new_kv = attend(att, count_gy, width, q_cols, key_cache, value_cache, own_y)
    new_kv = new_kv.reshape(rows_dev, 2 * HD)
    attended = back
    back = lax.all_to_all(back, "gy", 0, 0)

    gate_z, up_z = second(left_z, right_z, gate_z, up_z, attended)
    gate_y, up_y = second(left_y, right_y, gate_y, up_y, gate_z)
    gate_z, up_z = send(gate_z, ring_z(1)), send(up_z, ring_z(-1))
    gate_y, up_y = send(gate_y, ring_y(1)), send(up_y, ring_y(-1))
    total_z = total(own_z, left_z, right_z, gate_z, up_z, back)
    total_y = total(own_y, left_y, right_y, gate_y, up_y, back)

    attended = back[:, :rows_dev].reshape(CHUNK, q_cols)
    extra = back[:, rows_dev]
    n_off = count_gx * rows_dev
    sums_hid = back[:, 8:].transpose(1, 0, 2).reshape(count_gx, -1)
    offsets = extra[:, :n_off].reshape(count_gy, count_gx, rows_dev).transpose(0, 2, 1)
    offsets = offsets.reshape(CHUNK, count_gx)
    scale = extra[:, n_off : n_off + 3 * rows_dev].reshape(count_gy, 3, rows_dev)
    scale = add(scale[:, 0], scale[:, 1], scale[:, 2]).reshape(CHUNK, 1)

    att_z = q_cols // 2

    def column_sums(begin, end):
        return jnp.stack([sums_hid[:, begin:end], sums_hid[:, hid + begin : hid + end]])

    hidden_z = hidden(
        total_z[0], *send_direct(total_z, ring_y), offsets, column_sums(0, HID_Z), scale,
        attended[:, :att_z],
    )
    hidden_y = hidden(
        total_y[0], *send_direct(total_y, ring_z), offsets, column_sums(HID_Z, hid), scale,
        attended[:, att_z:],
    )

    def down(part, first, second, hid, att):
        inner = jnp.concatenate(gather_direct(part, first), axis=1)
        left = send(inner, second(1))
        right = send(inner, second(-1))
        low = send(left[0], second(1))
        high = send(right[1], second(-1))
        half = part.shape[2]

        def product(low, high):
            middle = hid.stop - hid.start - half
            out = dot(low, w_down[hid.start : hid.start + half])
            out = out + dot(high[:, :middle], w_down[hid.start + half : hid.stop])
            return out + dot(high[:, middle:], w_attn_out[att])

        return jnp.concatenate(
            [
                product(inner[0], inner[1]),
                product(right[0], right[1]),
                product(low, high),
                product(left[0], left[1]),
            ],
            axis=0,
        )

    down_z = down(hidden_z, ring_y, ring_z, slice(0, HID_Z), slice(0, att_z))
    down_y = down(hidden_y, ring_z, ring_y, slice(HID_Z, hid), slice(att_z, q_cols))
    d_out = w_down.shape[1]
    terms = down_z.reshape(NZ, NY, CHUNK, d_out)
    terms = terms + down_y.reshape(NY, NZ, CHUNK, d_out).transpose(1, 0, 2, 3)
    terms = roll(roll(terms.astype(BF16), 0, (NZ - z) % NZ), 1, (NY - y) % NY)

    terms = terms.reshape(NX, 2, -1, d_out)
    theirs = lax.dynamic_index_in_dim(terms, 1 - core, 1, keepdims=False)
    ours = lax.dynamic_index_in_dim(terms, core, 1, keepdims=False)
    ours = add(ours, send(theirs, CORES, "gy")).astype(BF16)
    ours = roll(ours, 0, x)
    branch = add(ours[0], *send_direct([ours[k] for k in range(NX)], ring_x, "gy"))
    layer_out = (tokens.astype(F32) + branch).astype(BF16)
    return (layer_out, new_kv)


def solution(mesh):
    return jax.shard_map(
        local,
        mesh=mesh,
        in_specs=(
            P("gy", "gx"),
            P("gx", "gy"),
            P("gx", "gy"),
            P("gx", "gy"),
            P("gx", "gy"),
            P("gy", "gx"),
            P("gy", "gx"),
            P(("gx", "gy"), None, None),
            P(("gx", "gy"), None, None),
        ),
        out_specs=(P("gy", "gx"), P(("gx", "gy"), None)),
        check_vma=False,
    )
```

```python
import functools

import jax
import jax.numpy as jnp
from jax import lax
from jax.experimental import pallas as pl
from jax.experimental.pallas import tpu as pltpu
from jax.sharding import PartitionSpec as P

D = 8192
HEADS = 32
HD = 256
NZ = 4
NY = 4
NX = 4
CHUNK = 32
QUARTER = 128
BLOCK = 512
HID_Z = 2048
ATT = 1152
FIRST_STAT = 64
SUMS_ATT = 384
SUMS_HID = 256
RIDE = SUMS_ATT + SUMS_HID
F32 = jnp.float32
BF16 = jnp.bfloat16
VMEM = pl.BlockSpec(memory_space=pltpu.VMEM)


def ring_y(shift):
    return [(z * NY + y, z * NY + (y + shift) % NY) for z in range(NZ) for y in range(NY)]


def ring_z(shift):
    return [(z * NY + y, ((z + shift) % NZ) * NY + y) for z in range(NZ) for y in range(NY)]


def ring_x(shift):
    return [(x * 2 + c, ((x + shift) % NX) * 2 + c) for x in range(NX) for c in range(2)]


CORES = [(x * 2 + c, x * 2 + 1 - c) for x in range(NX) for c in range(2)]


def send(value, pairs, axis="gx"):
    return lax.ppermute(value, axis, pairs)


def send_direct(chunks, ring, axis="gx"):
    return (
        send(chunks[1], ring(1), axis),
        send(chunks[3], ring(-1), axis),
        send(chunks[2], ring(2), axis),
    )


def gather_direct(value, ring, axis="gx"):
    left, right, far = send_direct([value] * 4, ring, axis)
    return [value, right, far, left]


def add(*values):
    total = values[0].astype(F32)
    for value in values[1:]:
        total = total + value.astype(F32)
    return total


def dot(a, b):
    return jnp.dot(a, b, preferred_element_type=F32)


def roll(values, axis, shift):
    size = values.shape[axis]
    return lax.dynamic_slice_in_dim(
        jnp.concatenate([values, values], axis=axis), shift, size, axis
    )


def shape(dims, dtype=BF16):
    return jax.ShapeDtypeStruct(dims, dtype)


def params(limit=10):
    return pltpu.CompilerParams(vmem_limit_bytes=limit * 1024 * 1024)


def prepare_kernel(place, strip, other, by_z, by_y, stats):
    z, y, x, core = place[0], place[1], place[2], place[3]
    for k in range(NX):
        chunk_z = lax.rem(x + k, NX)
        for source, owner in ((strip, core), (other, 1 - core)):
            for part in range(2):
                chunk_y = owner * 2 + part
                values = source[k, part * CHUNK : (part + 1) * CHUNK, :].astype(F32)
                mean = jnp.mean(values, axis=1, keepdims=True)
                centered = values - mean
                spread = jnp.sum(centered * centered, axis=1, keepdims=True)
                centered = centered.astype(BF16)
                away_z = lax.rem(chunk_z - z + NZ, NZ)
                away_y = lax.rem(chunk_y - y + NY, NY)
                to_z = lax.rem(away_z + 2, NZ) * NY + away_y
                to_y = lax.rem(away_y + 2, NY) * NZ + away_z
                by_z[pl.ds(pl.multiple_of(to_z * CHUNK, CHUNK), CHUNK), :] = centered
                by_y[pl.ds(pl.multiple_of(to_y * CHUNK, CHUNK), CHUNK), :] = centered
                lane = lax.broadcasted_iota(jnp.int32, (CHUNK, 128), 1)
                parts = jnp.zeros((CHUNK, 128), F32)
                for i, value in enumerate((mean, spread)):
                    for n in range(3):
                        piece = value.astype(BF16).astype(F32)
                        parts = jnp.where(lane == FIRST_STAT + 3 * i + n, piece, parts)
                        value = value - piece
                at = (chunk_z * NY + chunk_y) * (CHUNK // 4)
                stats[pl.ds(at, CHUNK // 4), :, :] = parts.astype(BF16).reshape(
                    CHUNK // 4, 4, 128
                )


def prepare(place, strip, other):
    width = strip.shape[2]
    rows = 2 * strip.shape[0] * strip.shape[1]
    return pl.pallas_call(
        prepare_kernel,
        in_specs=[pl.BlockSpec(memory_space=pltpu.SMEM), VMEM, VMEM],
        out_specs=[VMEM] * 3,
        out_shape=[shape((rows, width))] * 2 + [shape((rows // 4, 4, 128))],
        compiler_params=params(),
        name="prepare",
    )(place, strip, other)


def queries_kernel(place, rows, query, keyval, riders, stats, out):
    z, y = place[0], place[1]
    q_cols = query.shape[1]
    out[:, :, ATT - 128 : ATT] = stats[...]
    for weight, begin in ((query, 0), (keyval, q_cols)):
        part = dot(rows[...], weight[...]).astype(BF16)
        for k in range(NZ):
            for i in range(NY):
                chunk = lax.rem(z + k + 2, NZ) * NY + lax.rem(y + i, NY)
                at = (k * NY + i) * CHUNK
                values = part[at : at + CHUNK].reshape(CHUNK // 4, 4, weight.shape[1])
                out[pl.ds(chunk * (CHUNK // 4), CHUNK // 4), :, begin : begin + weight.shape[1]] = (
                    values
                )
    for n in range(0, out.shape[0], riders.shape[0]):
        at = slice(n, n + riders.shape[0])
        out[at, :, ATT:] = riders[...]


def queries(place, rows, query, keyval, riders, stats):
    return pl.pallas_call(
        queries_kernel,
        in_specs=[pl.BlockSpec(memory_space=pltpu.SMEM)] + [VMEM] * 5,
        out_specs=VMEM,
        out_shape=shape((rows.shape[0] // 4, 4, ATT + RIDE)),
        compiler_params=params(16),
        name="queries",
    )(place, rows, query, keyval, riders, stats)


def products_kernel(rows, gate, up, later, ahead, behind, gate_on, up_on, own):
    for i, weight in enumerate((gate, up)):
        out = dot(rows[...], weight[...]).astype(BF16)
        (ahead, behind)[i][i] = out[:QUARTER]
        own[i] = out[2 * QUARTER : 3 * QUARTER]
        if i == 0:
            behind[0] = out[QUARTER : 2 * QUARTER]
            gate_on[...] = out[3 * QUARTER :]
        else:
            up_on[...] = out[QUARTER : 2 * QUARTER]
            ahead[1] = out[3 * QUARTER :]


def products(rows, gate, up, begin, cols, later):
    width = rows.shape[1]
    skip = begin // BLOCK
    column = pl.BlockSpec((width, BLOCK), lambda j: (0, skip + j))
    flat = pl.BlockSpec((QUARTER, BLOCK), lambda j: (0, j))
    both = pl.BlockSpec((2, QUARTER, BLOCK), lambda j: (0, 0, j))
    return pl.pallas_call(
        products_kernel,
        grid=(cols // BLOCK,),
        in_specs=[pl.BlockSpec(rows.shape, lambda j: (0, 0)), column, column]
        + [pl.BlockSpec(memory_space=pl.ANY)],
        out_specs=[both] * 2 + [flat] * 2 + [both],
        out_shape=[shape((2, QUARTER, cols))] * 2
        + [shape((QUARTER, cols))] * 2
        + [shape((2, QUARTER, cols))],
        compiler_params=params(56),
        name="products",
    )(rows, gate, up, later)


def second_kernel(left, right, gate_in, up_in, later, gate, up):
    gate[...] = add(gate_in[...], left[0]).astype(BF16)
    up[...] = add(up_in[...], right[0]).astype(BF16)


def half(values, i):
    return pl.BlockSpec((1,) + values.shape[1:], lambda j: (i, 0, 0))


def whole(values):
    return pl.BlockSpec(values.shape, lambda j: (0,) * values.ndim)


def second(left, right, gate, up, later):
    return pl.pallas_call(
        second_kernel,
        grid=(1,),
        in_specs=[half(left, 0), half(right, 1), whole(gate), whole(up)]
        + [pl.BlockSpec(memory_space=pl.ANY)],
        out_specs=[whole(gate), whole(up)],
        out_shape=[shape(gate.shape)] * 2,
        compiler_params=params(10),
        name="second",
    )(left, right, gate, up, later)


def total_kernel(own, left, right, gate, up, later, *outs):
    for k, out in enumerate(outs):
        at = slice(k * CHUNK, (k + 1) * CHUNK)
        out[0] = add(own[0, at, :], gate[at, :], right[0, at, :]).astype(BF16)
        out[1] = add(own[1, at, :], left[0, at, :], up[at, :]).astype(BF16)


def total(own, left, right, gate, up, later):
    outs = [shape((2, CHUNK, own.shape[2]))] * 4
    return pl.pallas_call(
        total_kernel,
        grid=(1,),
        in_specs=[whole(own), half(left, 1), half(right, 0), whole(gate), whole(up)]
        + [pl.BlockSpec(memory_space=pl.ANY)],
        out_specs=[whole(out) for out in outs],
        out_shape=outs,
        compiler_params=params(56),
        name="total",
    )(own, left, right, gate, up, later)


def hidden_kernel(own, left, right, far, offsets, sums, scale, *refs):
    out = refs[-1]
    both = []
    for i in range(2):
        value = add(own[i], left[i], right[i], far[i]) + dot(offsets[...], sums[i])
        both.append(value * scale[...])
    gate, up = both
    joined = [(gate / (1.0 + jnp.exp(-gate)) * up).astype(BF16)]
    joined = jnp.concatenate(joined + [ref[...] for ref in refs[:-1]], axis=1)
    half = out.shape[2]
    out[0] = joined[:, :half]
    out[1] = joined[:, half:]


def hidden(own, left, right, far, offsets, sums, scale, *att):
    cols = own.shape[2] + sum(v.shape[1] for v in att)
    return pl.pallas_call(
        hidden_kernel,
        in_specs=[VMEM] * (7 + len(att)),
        out_specs=VMEM,
        out_shape=shape((2, CHUNK, cols // 2)),
        compiler_params=params(),
        name="hidden",
    )(own, left, right, far, offsets, sums, scale, *att)


def attend_kernel(come, turn, keys, values, later, back, new_kv, att, attended, *, width, q_cols):
    row = pl.program_id(0)
    blocks = come.shape[0] // back.shape[0]
    count = back.shape[0]
    rows = att.shape[0]
    heads = q_cols // HD
    half = HD // 2

    @pl.when(row == 0)
    def _():
        means, spreads = [], []
        for b in range(blocks):
            stats = come[b * count, :, ATT - 128 : ATT].astype(F32)
            at = [stats[:, FIRST_STAT + i : FIRST_STAT + i + 1] for i in range(6)]
            means.append(at[0] + at[1] + at[2])
            spreads.append(at[3] + at[4] + at[5])
        mean = sum(means[1:], means[0]) / blocks
        offsets = [value - mean for value in means]
        spread = sum(v + width * o * o for v, o in zip(spreads, offsets)) / D
        scale = lax.rsqrt(spread + 1e-05)
        total = jnp.zeros((count, rows, ATT), F32)
        for b in range(blocks):
            at = slice(b * count, (b + 1) * count)
            sums = jnp.concatenate(
                [come[at, i : i + 1, ATT : ATT + SUMS_ATT] for i in range(ATT // SUMS_ATT)], axis=2
            )
            total = total + come[at, :, :ATT].astype(F32) + offsets[b][None] * sums.astype(F32)
            back[:, 8 + b : 9 + b, :] = jnp.concatenate(
                [come[at, i : i + 1, ATT + SUMS_ATT :] for i in range(rows)], axis=2
            )
        total = (total * scale[None]).astype(BF16)
        for r in range(rows):
            att[r] = total[:, r, :]
        lane = lax.broadcasted_iota(jnp.int32, (rows, back.shape[2]), 1)
        line = lax.broadcasted_iota(jnp.int32, (rows, back.shape[2]), 0)
        pieces = list(offsets)
        rest = scale
        for _ in range(3):
            pieces.append(rest.astype(BF16).astype(F32))
            rest = rest - pieces[-1]
        extra = jnp.zeros(lane.shape, F32)
        for i, piece in enumerate(pieces):
            extra = extra + jnp.where(lane == i * rows + line, piece, 0.0)
        extra = jnp.sum(extra, axis=0, keepdims=True).astype(BF16)
        back[:, rows:8, :] = jnp.broadcast_to(extra[None], (count, 8 - rows, back.shape[2]))

    cos_part, sin_part = turn[0:1, :], turn[1:2, :]

    def rotated(v):
        first, second = v[:, :half], v[:, half:]
        return jnp.concatenate(
            [first * cos_part - second * sin_part, first * sin_part + second * cos_part], axis=1
        )

    mine = att[row].astype(F32)
    queries = jnp.concatenate([mine[:, h * HD : (h + 1) * HD] for h in range(heads)], axis=0)
    queries = (rotated(queries) * HD ** (-0.5)).astype(BF16)
    part = 2 * HD // count
    key = jnp.concatenate([mine[j : j + 1, q_cols : q_cols + part] for j in range(4)], axis=1)
    key = rotated(key).astype(BF16)
    value = jnp.concatenate([mine[j : j + 1, q_cols : q_cols + part] for j in range(4, 8)], axis=1)
    new_kv[0, :, :HD] = key
    new_kv[0, :, HD:] = value.astype(BF16)
    scores = lax.dot_general(
        queries, keys[0], (((1,), (1,)), ((), ())), preferred_element_type=F32
    )
    own = jnp.sum(queries.astype(F32) * key.astype(F32), axis=1, keepdims=True)
    top = jnp.maximum(jnp.max(scores, axis=1, keepdims=True), own)
    weights = jnp.exp(scores - top)
    own_w = jnp.exp(own - top)
    sums = jnp.sum(weights, axis=1, keepdims=True) + own_w
    probs = (weights / sums).astype(BF16)
    mixed = dot(probs, values[0]) + (own_w / sums).astype(BF16).astype(F32) * value
    for h in range(heads):
        attended[row, :, h * HD : (h + 1) * HD] = mixed[h * count : (h + 1) * count].astype(BF16)

    @pl.when(row == rows - 1)
    def _():
        for r in range(rows):
            back[:, r, :] = attended[r]


def attend(come, count, width, q_cols, key_cache, value_cache, later):
    half = HD // 2
    freqs = 10000.0 ** (-jnp.arange(half, dtype=F32) / half)
    angles = F32(key_cache.shape[1]) * freqs
    turn = jnp.stack([jnp.cos(angles), jnp.sin(angles)])
    rows = come.shape[1]
    blocks = come.shape[0] // count
    cache = pl.BlockSpec((1,) + key_cache.shape[1:], lambda r: (r, 0, 0))
    back = shape((count, 8 + blocks, q_cols))
    return pl.pallas_call(
        functools.partial(attend_kernel, width=width, q_cols=q_cols),
        grid=(rows,),
        in_specs=[whole(come), whole(turn), cache, cache, pl.BlockSpec(memory_space=pl.ANY)],
        out_specs=[whole(back), pl.BlockSpec((1, 1, 2 * HD), lambda r: (r, 0, 0))],
        out_shape=[back, shape((rows, 1, 2 * HD))],
        scratch_shapes=[
            pltpu.VMEM((rows, count, ATT), BF16),
            pltpu.VMEM((rows, count, q_cols), BF16),
        ],
        compiler_params=params(16),
        name="attend",
    )(come, turn, key_cache, value_cache, later)


def local(tokens, w_query, w_key_value, w_gate, w_up, w_attn_out, w_down, key_cache, value_cache):
    count_gx = lax.axis_size("gx")
    count_gy = lax.axis_size("gy")
    mine = lax.axis_index("gx")
    place = lax.axis_index("gy")
    z, y = mine // NY, mine % NY
    x, core = place // 2, place % 2
    width = tokens.shape[1]
    q_cols = w_query.shape[1]
    att_cols = q_cols + w_key_value.shape[1]
    hid = w_gate.shape[1]
    hid_y = hid - HID_Z
    rows_dev = CHUNK // count_gy

    ones = jnp.ones((8, width), BF16)
    sums = [dot(ones, w)[:1].astype(BF16) for w in (w_query, w_key_value, w_gate, w_up)]
    sums_att = jnp.pad(jnp.concatenate(sums[:2], axis=1), ((0, 0), (0, 4 * SUMS_ATT - att_cols)))
    sums_att = jnp.broadcast_to(sums_att.reshape(1, 4, SUMS_ATT), (count_gy, 4, SUMS_ATT))
    sums_hid = jnp.concatenate(sums[2:], axis=1).reshape(count_gy, 4, SUMS_HID)
    riders = jnp.concatenate([sums_att, sums_hid], axis=2)

    position = jnp.stack([z, y, x, core]).astype(jnp.int32)
    strip = jnp.stack(gather_direct(tokens, ring_x, "gy"))
    other = send(strip, CORES, "gy")
    by_z, by_y, stats = prepare(position, strip, other)

    att = queries(position, by_z, w_query, w_key_value, riders, stats)
    later = att
    att = lax.all_to_all(att, ("gx", "gy"), 0, 0)

    ahead_z, behind_z, gate_z, up_z, own_z = products(by_z, w_gate, w_up, 0, HID_Z, later)
    ahead_y, behind_y, gate_y, up_y, own_y = products(by_y, w_gate, w_up, HID_Z, hid_y, own_z)
    left_z = send(ahead_z, ring_z(1))
    right_z = send(behind_z, ring_z(-1))
    left_y = send(ahead_y, ring_y(1))
    right_y = send(behind_y, ring_y(-1))

    back, new_kv = attend(att, count_gy, width, q_cols, key_cache, value_cache, own_y)
    new_kv = new_kv.reshape(rows_dev, 2 * HD)
    attended = back
    back = lax.all_to_all(back, "gy", 0, 0)

    gate_z, up_z = second(left_z, right_z, gate_z, up_z, attended)
    gate_y, up_y = second(left_y, right_y, gate_y, up_y, gate_z)
    gate_z, up_z = send(gate_z, ring_z(1)), send(up_z, ring_z(-1))
    gate_y, up_y = send(gate_y, ring_y(1)), send(up_y, ring_y(-1))
    total_z = total(own_z, left_z, right_z, gate_z, up_z, back)
    total_y = total(own_y, left_y, right_y, gate_y, up_y, back)

    attended = back[:, :rows_dev].reshape(CHUNK, q_cols)
    extra = back[:, rows_dev]
    n_off = count_gx * rows_dev
    sums_hid = back[:, 8:].transpose(1, 0, 2).reshape(count_gx, -1)
    offsets = extra[:, :n_off].reshape(count_gy, count_gx, rows_dev).transpose(0, 2, 1)
    offsets = offsets.reshape(CHUNK, count_gx)
    scale = extra[:, n_off : n_off + 3 * rows_dev].reshape(count_gy, 3, rows_dev)
    scale = add(scale[:, 0], scale[:, 1], scale[:, 2]).reshape(CHUNK, 1)

    att_z = q_cols // 2

    def column_sums(begin, end):
        return jnp.stack([sums_hid[:, begin:end], sums_hid[:, hid + begin : hid + end]])

    hidden_z = hidden(
        total_z[0], *send_direct(total_z, ring_y), offsets, column_sums(0, HID_Z), scale,
        attended[:, :att_z],
    )
    hidden_y = hidden(
        total_y[0], *send_direct(total_y, ring_z), offsets, column_sums(HID_Z, hid), scale,
        attended[:, att_z:],
    )

    def down(part, first, second, hid, att):
        inner = jnp.concatenate(gather_direct(part, first), axis=1)
        left = send(inner, second(1))
        right = send(inner, second(-1))
        low = send(left[0], second(1))
        high = send(right[1], second(-1))
        half = part.shape[2]

        def product(low, high):
            middle = hid.stop - hid.start - half
            out = dot(low, w_down[hid.start : hid.start + half])
            out = out + dot(high[:, :middle], w_down[hid.start + half : hid.stop])
            return out + dot(high[:, middle:], w_attn_out[att])

        return jnp.concatenate(
            [
                product(inner[0], inner[1]),
                product(right[0], right[1]),
                product(low, high),
                product(left[0], left[1]),
            ],
            axis=0,
        )

    down_z = down(hidden_z, ring_y, ring_z, slice(0, HID_Z), slice(0, att_z))
    down_y = down(hidden_y, ring_z, ring_y, slice(HID_Z, hid), slice(att_z, q_cols))
    d_out = w_down.shape[1]
    terms = down_z.reshape(NZ, NY, CHUNK, d_out)
    terms = terms + down_y.reshape(NY, NZ, CHUNK, d_out).transpose(1, 0, 2, 3)
    terms = roll(roll(terms.astype(BF16), 0, (NZ - z) % NZ), 1, (NY - y) % NY)

    terms = terms.reshape(NX, 2, -1, d_out)
    theirs = lax.dynamic_index_in_dim(terms, 1 - core, 1, keepdims=False)
    ours = lax.dynamic_index_in_dim(terms, core, 1, keepdims=False)
    ours = add(ours, send(theirs, CORES, "gy")).astype(BF16)
    ours = roll(ours, 0, x)
    branch = add(ours[0], *send_direct([ours[k] for k in range(NX)], ring_x, "gy"))
    layer_out = (tokens.astype(F32) + branch).astype(BF16)
    return (layer_out, new_kv)


def solution(mesh):
    return jax.shard_map(
        local,
        mesh=mesh,
        in_specs=(
            P("gy", "gx"),
            P("gx", "gy"),
            P("gx", "gy"),
            P("gx", "gy"),
            P("gx", "gy"),
            P("gy", "gx"),
            P("gy", "gx"),
            P(("gx", "gy"), None, None),
            P(("gx", "gy"), None, None),
        ),
        out_specs=(P("gy", "gx"), P(("gx", "gy"), None)),
        check_vma=False,
    )
```

```python
import functools

import jax
import jax.numpy as jnp
from jax import lax
from jax.experimental import pallas as pl
from jax.experimental.pallas import tpu as pltpu
from jax.sharding import PartitionSpec as P

D = 8192
HEADS = 32
HD = 256
NZ = 4
NY = 4
NX = 4
CHUNK = 32
QUARTER = 128
BLOCK = 512
HID_Z = 2048
ATT = 1152
FIRST_STAT = 64
SUMS_ATT = 384
SUMS_HID = 256
RIDE = SUMS_ATT + SUMS_HID
F32 = jnp.float32
BF16 = jnp.bfloat16
VMEM = pl.BlockSpec(memory_space=pltpu.VMEM)


def ring_y(shift):
    return [(z * NY + y, z * NY + (y + shift) % NY) for z in range(NZ) for y in range(NY)]


def ring_z(shift):
    return [(z * NY + y, ((z + shift) % NZ) * NY + y) for z in range(NZ) for y in range(NY)]


def ring_x(shift):
    return [(x * 2 + c, ((x + shift) % NX) * 2 + c) for x in range(NX) for c in range(2)]


CORES = [(x * 2 + c, x * 2 + 1 - c) for x in range(NX) for c in range(2)]


def send(value, pairs, axis="gx"):
    return lax.ppermute(value, axis, pairs)


def send_direct(chunks, ring, axis="gx"):
    return (
        send(chunks[1], ring(1), axis),
        send(chunks[3], ring(-1), axis),
        send(chunks[2], ring(2), axis),
    )


def gather_direct(value, ring, axis="gx"):
    left, right, far = send_direct([value] * 4, ring, axis)
    return [value, right, far, left]


def add(*values):
    total = values[0].astype(F32)
    for value in values[1:]:
        total = total + value.astype(F32)
    return total


def dot(a, b):
    return jnp.dot(a, b, preferred_element_type=F32)


def roll(values, axis, shift):
    size = values.shape[axis]
    return lax.dynamic_slice_in_dim(
        jnp.concatenate([values, values], axis=axis), shift, size, axis
    )


def shape(dims, dtype=BF16):
    return jax.ShapeDtypeStruct(dims, dtype)


def params(limit=10):
    return pltpu.CompilerParams(vmem_limit_bytes=limit * 1024 * 1024)


def prepare_kernel(place, strip, other, by_z, by_y, stats):
    z, y, x, core = place[0], place[1], place[2], place[3]
    for k in range(NX):
        chunk_z = lax.rem(x + k, NX)
        for source, owner in ((strip, core), (other, 1 - core)):
            for part in range(2):
                chunk_y = owner * 2 + part
                values = source[k, part * CHUNK : (part + 1) * CHUNK, :].astype(F32)
                mean = jnp.mean(values, axis=1, keepdims=True)
                centered = values - mean
                spread = jnp.sum(centered * centered, axis=1, keepdims=True)
                centered = centered.astype(BF16)
                away_z = lax.rem(chunk_z - z + NZ, NZ)
                away_y = lax.rem(chunk_y - y + NY, NY)
                to_z = lax.rem(away_z + 2, NZ) * NY + away_y
                to_y = lax.rem(away_y + 2, NY) * NZ + away_z
                by_z[pl.ds(pl.multiple_of(to_z * CHUNK, CHUNK), CHUNK), :] = centered
                by_y[pl.ds(pl.multiple_of(to_y * CHUNK, CHUNK), CHUNK), :] = centered
                lane = lax.broadcasted_iota(jnp.int32, (CHUNK, 128), 1)
                parts = jnp.zeros((CHUNK, 128), F32)
                for i, value in enumerate((mean, spread)):
                    for n in range(3):
                        piece = value.astype(BF16).astype(F32)
                        parts = jnp.where(lane == FIRST_STAT + 3 * i + n, piece, parts)
                        value = value - piece
                at = (chunk_z * NY + chunk_y) * (CHUNK // 4)
                stats[pl.ds(at, CHUNK // 4), :, :] = parts.astype(BF16).reshape(
                    CHUNK // 4, 4, 128
                )


def prepare(place, strip, other):
    width = strip.shape[2]
    rows = 2 * strip.shape[0] * strip.shape[1]
    return pl.pallas_call(
        prepare_kernel,
        in_specs=[pl.BlockSpec(memory_space=pltpu.SMEM), VMEM, VMEM],
        out_specs=[VMEM] * 3,
        out_shape=[shape((rows, width))] * 2 + [shape((rows // 4, 4, 128))],
        compiler_params=params(56),
        name="prepare",
    )(place, strip, other)


def queries_kernel(place, rows, query, keyval, riders, stats, out):
    z, y = place[0], place[1]
    q_cols = query.shape[1]
    out[:, :, ATT - 128 : ATT] = stats[...]
    for weight, begin in ((query, 0), (keyval, q_cols)):
        part = dot(rows[...], weight[...]).astype(BF16)
        for k in range(NZ):
            for i in range(NY):
                chunk = lax.rem(z + k + 2, NZ) * NY + lax.rem(y + i, NY)
                at = (k * NY + i) * CHUNK
                values = part[at : at + CHUNK].reshape(CHUNK // 4, 4, weight.shape[1])
                out[pl.ds(chunk * (CHUNK // 4), CHUNK // 4), :, begin : begin + weight.shape[1]] = (
                    values
                )
    for n in range(0, out.shape[0], riders.shape[0]):
        at = slice(n, n + riders.shape[0])
        out[at, :, ATT:] = riders[...]


def queries(place, rows, query, keyval, riders, stats):
    return pl.pallas_call(
        queries_kernel,
        in_specs=[pl.BlockSpec(memory_space=pltpu.SMEM)] + [VMEM] * 5,
        out_specs=VMEM,
        out_shape=shape((rows.shape[0] // 4, 4, ATT + RIDE)),
        compiler_params=params(16),
        name="queries",
    )(place, rows, query, keyval, riders, stats)


def products_kernel(rows, gate, up, later, ahead, behind, gate_on, up_on, own):
    for i, weight in enumerate((gate, up)):
        out = dot(rows[...], weight[...]).astype(BF16)
        (ahead, behind)[i][i] = out[:QUARTER]
        own[i] = out[2 * QUARTER : 3 * QUARTER]
        if i == 0:
            behind[0] = out[QUARTER : 2 * QUARTER]
            gate_on[...] = out[3 * QUARTER :]
        else:
            up_on[...] = out[QUARTER : 2 * QUARTER]
            ahead[1] = out[3 * QUARTER :]


def products(rows, gate, up, begin, cols, later):
    width = rows.shape[1]
    skip = begin // BLOCK
    column = pl.BlockSpec((width, BLOCK), lambda j: (0, skip + j))
    flat = pl.BlockSpec((QUARTER, BLOCK), lambda j: (0, j))
    both = pl.BlockSpec((2, QUARTER, BLOCK), lambda j: (0, 0, j))
    return pl.pallas_call(
        products_kernel,
        grid=(cols // BLOCK,),
        in_specs=[pl.BlockSpec(rows.shape, lambda j: (0, 0)), column, column]
        + [pl.BlockSpec(memory_space=pl.ANY)],
        out_specs=[both] * 2 + [flat] * 2 + [both],
        out_shape=[shape((2, QUARTER, cols))] * 2
        + [shape((QUARTER, cols))] * 2
        + [shape((2, QUARTER, cols))],
        compiler_params=params(56),
        name="products",
    )(rows, gate, up, later)


def second_kernel(left, right, gate_in, up_in, later, gate, up):
    gate[...] = add(gate_in[...], left[0]).astype(BF16)
    up[...] = add(up_in[...], right[0]).astype(BF16)


def half(values, i):
    return pl.BlockSpec((1,) + values.shape[1:], lambda j: (i, 0, 0))


def whole(values):
    return pl.BlockSpec(values.shape, lambda j: (0,) * values.ndim)


def second(left, right, gate, up, later):
    return pl.pallas_call(
        second_kernel,
        grid=(1,),
        in_specs=[half(left, 0), half(right, 1), whole(gate), whole(up)]
        + [pl.BlockSpec(memory_space=pl.ANY)],
        out_specs=[whole(gate), whole(up)],
        out_shape=[shape(gate.shape)] * 2,
        compiler_params=params(10),
        name="second",
    )(left, right, gate, up, later)


def total_kernel(own, left, right, gate, up, later, *outs):
    for k, out in enumerate(outs):
        at = slice(k * CHUNK, (k + 1) * CHUNK)
        out[0] = add(own[0, at, :], gate[at, :], right[0, at, :]).astype(BF16)
        out[1] = add(own[1, at, :], left[0, at, :], up[at, :]).astype(BF16)


def total(own, left, right, gate, up, later):
    outs = [shape((2, CHUNK, own.shape[2]))] * 4
    return pl.pallas_call(
        total_kernel,
        grid=(1,),
        in_specs=[whole(own), half(left, 1), half(right, 0), whole(gate), whole(up)]
        + [pl.BlockSpec(memory_space=pl.ANY)],
        out_specs=[whole(out) for out in outs],
        out_shape=outs,
        compiler_params=params(56),
        name="total",
    )(own, left, right, gate, up, later)


def hidden_kernel(own, left, right, far, offsets, sums, scale, *refs):
    out = refs[-1]
    both = []
    for i in range(2):
        value = add(own[i], left[i], right[i], far[i]) + dot(offsets[...], sums[i])
        both.append(value * scale[...])
    gate, up = both
    joined = [(gate / (1.0 + jnp.exp(-gate)) * up).astype(BF16)]
    joined = jnp.concatenate(joined + [ref[...] for ref in refs[:-1]], axis=1)
    half = out.shape[2]
    out[0] = joined[:, :half]
    out[1] = joined[:, half:]


def hidden(own, left, right, far, offsets, sums, scale, *att):
    cols = own.shape[2] + sum(v.shape[1] for v in att)
    return pl.pallas_call(
        hidden_kernel,
        in_specs=[VMEM] * (7 + len(att)),
        out_specs=VMEM,
        out_shape=shape((2, CHUNK, cols // 2)),
        compiler_params=params(),
        name="hidden",
    )(own, left, right, far, offsets, sums, scale, *att)


def attend_kernel(come, turn, keys, values, later, back, new_kv, att, attended, *, width, q_cols):
    row = pl.program_id(0)
    blocks = come.shape[0] // back.shape[0]
    count = back.shape[0]
    rows = att.shape[0]
    heads = q_cols // HD
    half = HD // 2

    @pl.when(row == 0)
    def _():
        means, spreads = [], []
        for b in range(blocks):
            stats = come[b * count, :, ATT - 128 : ATT].astype(F32)
            at = [stats[:, FIRST_STAT + i : FIRST_STAT + i + 1] for i in range(6)]
            means.append(at[0] + at[1] + at[2])
            spreads.append(at[3] + at[4] + at[5])
        mean = sum(means[1:], means[0]) / blocks
        offsets = [value - mean for value in means]
        spread = sum(v + width * o * o for v, o in zip(spreads, offsets)) / D
        scale = lax.rsqrt(spread + 1e-05)
        total = jnp.zeros((count, rows, ATT), F32)
        for b in range(blocks):
            at = slice(b * count, (b + 1) * count)
            sums = jnp.concatenate(
                [come[at, i : i + 1, ATT : ATT + SUMS_ATT] for i in range(ATT // SUMS_ATT)], axis=2
            )
            total = total + come[at, :, :ATT].astype(F32) + offsets[b][None] * sums.astype(F32)
            back[:, 8 + b : 9 + b, :] = jnp.concatenate(
                [come[at, i : i + 1, ATT + SUMS_ATT :] for i in range(rows)], axis=2
            )
        total = (total * scale[None]).astype(BF16)
        for r in range(rows):
            att[r] = total[:, r, :]
        lane = lax.broadcasted_iota(jnp.int32, (rows, back.shape[2]), 1)
        line = lax.broadcasted_iota(jnp.int32, (rows, back.shape[2]), 0)
        pieces = list(offsets)
        rest = scale
        for _ in range(3):
            pieces.append(rest.astype(BF16).astype(F32))
            rest = rest - pieces[-1]
        extra = jnp.zeros(lane.shape, F32)
        for i, piece in enumerate(pieces):
            extra = extra + jnp.where(lane == i * rows + line, piece, 0.0)
        extra = jnp.sum(extra, axis=0, keepdims=True).astype(BF16)
        back[:, rows:8, :] = jnp.broadcast_to(extra[None], (count, 8 - rows, back.shape[2]))

    cos_part, sin_part = turn[0:1, :], turn[1:2, :]

    def rotated(v):
        first, second = v[:, :half], v[:, half:]
        return jnp.concatenate(
            [first * cos_part - second * sin_part, first * sin_part + second * cos_part], axis=1
        )

    mine = att[row].astype(F32)
    queries = jnp.concatenate([mine[:, h * HD : (h + 1) * HD] for h in range(heads)], axis=0)
    queries = (rotated(queries) * HD ** (-0.5)).astype(BF16)
    part = 2 * HD // count
    key = jnp.concatenate([mine[j : j + 1, q_cols : q_cols + part] for j in range(4)], axis=1)
    key = rotated(key).astype(BF16)
    value = jnp.concatenate([mine[j : j + 1, q_cols : q_cols + part] for j in range(4, 8)], axis=1)
    new_kv[0, :, :HD] = key
    new_kv[0, :, HD:] = value.astype(BF16)
    scores = lax.dot_general(
        queries, keys[0], (((1,), (1,)), ((), ())), preferred_element_type=F32
    )
    own = jnp.sum(queries.astype(F32) * key.astype(F32), axis=1, keepdims=True)
    top = jnp.maximum(jnp.max(scores, axis=1, keepdims=True), own)
    weights = jnp.exp(scores - top)
    own_w = jnp.exp(own - top)
    sums = jnp.sum(weights, axis=1, keepdims=True) + own_w
    probs = (weights / sums).astype(BF16)
    mixed = dot(probs, values[0]) + (own_w / sums).astype(BF16).astype(F32) * value
    for h in range(heads):
        attended[row, :, h * HD : (h + 1) * HD] = mixed[h * count : (h + 1) * count].astype(BF16)

    @pl.when(row == rows - 1)
    def _():
        for r in range(rows):
            back[:, r, :] = attended[r]


def attend(come, count, width, q_cols, key_cache, value_cache, later):
    half = HD // 2
    freqs = 10000.0 ** (-jnp.arange(half, dtype=F32) / half)
    angles = F32(key_cache.shape[1]) * freqs
    turn = jnp.stack([jnp.cos(angles), jnp.sin(angles)])
    rows = come.shape[1]
    blocks = come.shape[0] // count
    cache = pl.BlockSpec((1,) + key_cache.shape[1:], lambda r: (r, 0, 0))
    back = shape((count, 8 + blocks, q_cols))
    return pl.pallas_call(
        functools.partial(attend_kernel, width=width, q_cols=q_cols),
        grid=(rows,),
        in_specs=[whole(come), whole(turn), cache, cache, pl.BlockSpec(memory_space=pl.ANY)],
        out_specs=[whole(back), pl.BlockSpec((1, 1, 2 * HD), lambda r: (r, 0, 0))],
        out_shape=[back, shape((rows, 1, 2 * HD))],
        scratch_shapes=[
            pltpu.VMEM((rows, count, ATT), BF16),
            pltpu.VMEM((rows, count, q_cols), BF16),
        ],
        compiler_params=params(16),
        name="attend",
    )(come, turn, key_cache, value_cache, later)


def local(tokens, w_query, w_key_value, w_gate, w_up, w_attn_out, w_down, key_cache, value_cache):
    count_gx = lax.axis_size("gx")
    count_gy = lax.axis_size("gy")
    mine = lax.axis_index("gx")
    place = lax.axis_index("gy")
    z, y = mine // NY, mine % NY
    x, core = place // 2, place % 2
    width = tokens.shape[1]
    q_cols = w_query.shape[1]
    att_cols = q_cols + w_key_value.shape[1]
    hid = w_gate.shape[1]
    hid_y = hid - HID_Z
    rows_dev = CHUNK // count_gy

    ones = jnp.ones((8, width), BF16)
    sums = [dot(ones, w)[:1].astype(BF16) for w in (w_query, w_key_value, w_gate, w_up)]
    sums_att = jnp.pad(jnp.concatenate(sums[:2], axis=1), ((0, 0), (0, 4 * SUMS_ATT - att_cols)))
    sums_att = jnp.broadcast_to(sums_att.reshape(1, 4, SUMS_ATT), (count_gy, 4, SUMS_ATT))
    sums_hid = jnp.concatenate(sums[2:], axis=1).reshape(count_gy, 4, SUMS_HID)
    riders = jnp.concatenate([sums_att, sums_hid], axis=2)

    position = jnp.stack([z, y, x, core]).astype(jnp.int32)
    strip = jnp.stack(gather_direct(tokens, ring_x, "gy"))
    other = send(strip, CORES, "gy")
    by_z, by_y, stats = prepare(position, strip, other)

    att = queries(position, by_z, w_query, w_key_value, riders, stats)
    later = att
    att = lax.all_to_all(att, ("gx", "gy"), 0, 0)

    ahead_z, behind_z, gate_z, up_z, own_z = products(by_z, w_gate, w_up, 0, HID_Z, later)
    ahead_y, behind_y, gate_y, up_y, own_y = products(by_y, w_gate, w_up, HID_Z, hid_y, own_z)
    left_z = send(ahead_z, ring_z(1))
    right_z = send(behind_z, ring_z(-1))
    left_y = send(ahead_y, ring_y(1))
    right_y = send(behind_y, ring_y(-1))

    back, new_kv = attend(att, count_gy, width, q_cols, key_cache, value_cache, own_y)
    new_kv = new_kv.reshape(rows_dev, 2 * HD)
    attended = back
    back = lax.all_to_all(back, "gy", 0, 0)

    gate_z, up_z = second(left_z, right_z, gate_z, up_z, attended)
    gate_y, up_y = second(left_y, right_y, gate_y, up_y, gate_z)
    gate_z, up_z = send(gate_z, ring_z(1)), send(up_z, ring_z(-1))
    gate_y, up_y = send(gate_y, ring_y(1)), send(up_y, ring_y(-1))
    total_z = total(own_z, left_z, right_z, gate_z, up_z, back)
    total_y = total(own_y, left_y, right_y, gate_y, up_y, back)

    attended = back[:, :rows_dev].reshape(CHUNK, q_cols)
    extra = back[:, rows_dev]
    n_off = count_gx * rows_dev
    sums_hid = back[:, 8:].transpose(1, 0, 2).reshape(count_gx, -1)
    offsets = extra[:, :n_off].reshape(count_gy, count_gx, rows_dev).transpose(0, 2, 1)
    offsets = offsets.reshape(CHUNK, count_gx)
    scale = extra[:, n_off : n_off + 3 * rows_dev].reshape(count_gy, 3, rows_dev)
    scale = add(scale[:, 0], scale[:, 1], scale[:, 2]).reshape(CHUNK, 1)

    att_z = q_cols // 2

    def column_sums(begin, end):
        return jnp.stack([sums_hid[:, begin:end], sums_hid[:, hid + begin : hid + end]])

    hidden_z = hidden(
        total_z[0], *send_direct(total_z, ring_y), offsets, column_sums(0, HID_Z), scale,
        attended[:, :att_z],
    )
    hidden_y = hidden(
        total_y[0], *send_direct(total_y, ring_z), offsets, column_sums(HID_Z, hid), scale,
        attended[:, att_z:],
    )

    def down(part, first, second, hid, att):
        inner = jnp.concatenate(gather_direct(part, first), axis=1)
        left = send(inner, second(1))
        right = send(inner, second(-1))
        low = send(left[0], second(1))
        high = send(right[1], second(-1))
        half = part.shape[2]

        def product(low, high):
            middle = hid.stop - hid.start - half
            out = dot(low, w_down[hid.start : hid.start + half])
            out = out + dot(high[:, :middle], w_down[hid.start + half : hid.stop])
            return out + dot(high[:, middle:], w_attn_out[att])

        return jnp.concatenate(
            [
                product(inner[0], inner[1]),
                product(right[0], right[1]),
                product(low, high),
                product(left[0], left[1]),
            ],
            axis=0,
        )

    down_z = down(hidden_z, ring_y, ring_z, slice(0, HID_Z), slice(0, att_z))
    down_y = down(hidden_y, ring_z, ring_y, slice(HID_Z, hid), slice(att_z, q_cols))
    d_out = w_down.shape[1]
    terms = down_z.reshape(NZ, NY, CHUNK, d_out)
    terms = terms + down_y.reshape(NY, NZ, CHUNK, d_out).transpose(1, 0, 2, 3)
    terms = roll(roll(terms.astype(BF16), 0, (NZ - z) % NZ), 1, (NY - y) % NY)

    terms = terms.reshape(NX, 2, -1, d_out)
    theirs = lax.dynamic_index_in_dim(terms, 1 - core, 1, keepdims=False)
    ours = lax.dynamic_index_in_dim(terms, core, 1, keepdims=False)
    ours = add(ours, send(theirs, CORES, "gy")).astype(BF16)
    ours = roll(ours, 0, x)
    branch = add(ours[0], *send_direct([ours[k] for k in range(NX)], ring_x, "gy"))
    layer_out = (tokens.astype(F32) + branch).astype(BF16)
    return (layer_out, new_kv)


def solution(mesh):
    return jax.shard_map(
        local,
        mesh=mesh,
        in_specs=(
            P("gy", "gx"),
            P("gx", "gy"),
            P("gx", "gy"),
            P("gx", "gy"),
            P("gx", "gy"),
            P("gy", "gx"),
            P("gy", "gx"),
            P(("gx", "gy"), None, None),
            P(("gx", "gy"), None, None),
        ),
        out_specs=(P("gy", "gx"), P(("gx", "gy"), None)),
        check_vma=False,
    )
```
